128 devices in a mesh: lon: 16 (over y_lo, x, core), lat: 8 (over y_hi, z).
Axes of the slice: x: 4, y: 4 (y_hi: 2, y_lo: 2; y = y_hi * 2 + y_lo), z: 4, core: 2. Of those that a mesh axis runs over, the one named last changes fastest.
Arguments:
- u_wind: float32 [16, 2880, 1024], P(None, 'lon', 'lat'), may hold values from -6 to 6
- v_wind: float32 [16, 2880, 1024], P(None, 'lon', 'lat'), may hold values from -6 to 6
- height: float32 [16, 2880, 1024], P(None, 'lon', 'lat'), may hold values from -6 to 6
Outputs:
- u_next: float32 [16, 2880, 1024], P(None, 'lon', 'lat')
- v_next: float32 [16, 2880, 1024], P(None, 'lon', 'lat')
- height_next: float32 [16, 2880, 1024], P(None, 'lon', 'lat')
The draws below stay inside these ranges and needn't reach their ends.
All inputs are finite; a program needn't handle non-finite values.
Results may differ from the reference program's by a relative error of at most 0.00013.
Values sent between devices are 32-bit elements; how exact they have to be, the bound alone decides.
No kernel may reach another device: no remote copies, remote signals or barrier semaphores. Data moves between devices by JAX's collectives and lax.ppermute only.
A program may use at most 192 MiB of HBM per device.

```python
import math
import jax
import jax.numpy as jnp

NLON = 2880
LEV = 16
NLAT = 1024


def steps_of(own_key, extent, split, low, largest):
    gain = 1.0
    for position, shards_of in split:
        draws = jax.random.uniform(jax.random.fold_in(jax.random.fold_in(own_key, 6), position), (shards_of,), jnp.float32, low / len(split), largest / len(split))
        gain = gain * jnp.repeat(jnp.exp(draws), extent[position] // shards_of).reshape((-1,) + (1,) * (len(extent) - 1 - position))
    return gain


def noise(stream_key, shape, deviation, most, shards=(), held_as=jnp.bfloat16):
    level = steps_of(stream_key, shape, shards, -0.22, 0.18) if shards else 1.0
    result = jax.random.normal(stream_key, shape, jnp.float32) * deviation * level
    return jnp.minimum(jnp.maximum(result, -most), most).astype(held_as)


def setup_inputs(seed: int = 0) -> dict:
    seeds = jax.random.split(jax.random.key(seed), 4)
    u_wind = noise(seeds[0], (LEV, NLON, NLAT), 1.0, 6.0, ((1, 16), (2, 8)), jnp.float32)
    v_wind = noise(seeds[1], (LEV, NLON, NLAT), 1.0, 6.0, ((1, 16), (2, 8)), jnp.float32)
    height = noise(seeds[2], (LEV, NLON, NLAT), 1.0, 6.0, ((1, 16), (2, 8)), jnp.float32)
    return dict(u_wind=u_wind, v_wind=v_wind, height=height)


grav_zonal = 0.3
grav_merid = 0.6
coriolis = 0.8
divergence_coef = 0.3
diffusion = 0.08


def shifted(field, row_step, col_step, row_count, col_count):
    return field[:, 1 + row_step:1 + row_step + row_count, 1 + col_step:1 + col_step + col_count]


def stencil(padded, first_row, lat_total):
    row_count = padded.shape[2] - 2
    col_count = padded.shape[3] - 2
    height, u_wind, v_wind = padded[0], padded[1], padded[2]

    def view(field, row_step, col_step):
        return shifted(field, row_step, col_step, row_count, col_count)

    def laplace(field):
        return view(field, 0, 1) + view(field, 0, -1) + view(field, 1, 0) + view(field, -1, 0) - 4.0 * view(field, 0, 0)

    lat_index = (first_row + jnp.arange(row_count)).astype(jnp.float32)[:, None]
    center = (lat_index + 0.5) * (math.pi / lat_total)
    cos_center = jnp.sin(center)
    sin_center = -jnp.cos(center)
    face = (lat_index + 1.0) * (math.pi / lat_total)
    sin_face = -jnp.cos(face)
    cos_face = jnp.where(lat_index + 1.0 < lat_total, jnp.sin(face), 0.0)
    cos_south = jnp.sin(lat_index * (math.pi / lat_total))
    u_next = (view(u_wind, 0, 0) - grav_zonal * (view(height, 0, 1) - view(height, 0, 0)) / cos_center
              + coriolis * sin_center * 0.25 * (view(v_wind, 0, 0) + view(v_wind, 0, 1) + view(v_wind, -1, 0) + view(v_wind, -1, 1))
              + diffusion * laplace(u_wind))
    v_next = (view(v_wind, 0, 0) - grav_merid * (view(height, 1, 0) - view(height, 0, 0))
              - coriolis * sin_face * 0.25 * (view(u_wind, 0, 0) + view(u_wind, 0, -1) + view(u_wind, 1, 0) + view(u_wind, 1, -1))
              + diffusion * laplace(v_wind))
    flux = (view(u_wind, 0, 0) - view(u_wind, 0, -1)) + cos_face * view(v_wind, 0, 0) - cos_south * view(v_wind, -1, 0)
    height_next = view(height, 0, 0) - divergence_coef * flux / cos_center + diffusion * laplace(height)
    return jnp.stack([height_next, u_next, v_next])


def lon_pad(field):
    return jnp.concatenate([field[..., -1:], field, field[..., :1]], -1)


def polar_filter(field):
    lon_total = field.shape[-1]
    spectra = jnp.fft.rfft(field, axis=-1)
    wavenum = jnp.arange(lon_total // 2 + 1).astype(jnp.float32)
    sine_vals = jnp.sin(wavenum * (math.pi / lon_total))
    sine_sq = sine_vals * sine_vals
    lat_index = jnp.arange(NLAT).astype(jnp.float32)
    cosine = jnp.sin((lat_index + 0.5) * (math.pi / NLAT))
    damp_ratio = (2.0 * cosine * cosine)[:, None]
    damping = damp_ratio / jnp.maximum(sine_sq[None, :], damp_ratio)
    smoothed = jnp.fft.irfft(spectra * damping, n=lon_total, axis=-1).astype(field.dtype)
    row_index = jnp.arange(NLAT)
    is_polar = (row_index < NLAT // 4) | (row_index >= NLAT - NLAT // 4)
    return jnp.where(is_polar[:, None], smoothed, field)


def reference(u_wind, v_wind, height):
    u_wind = jnp.swapaxes(u_wind, 1, 2)
    v_wind = jnp.swapaxes(v_wind, 1, 2)
    height = jnp.swapaxes(height, 1, 2)
    half_lon = NLON // 2
    h_pad, u_pad, v_pad = lon_pad(height), lon_pad(u_wind), lon_pad(v_wind)
    h_turn = lon_pad(jnp.roll(height, -half_lon, axis=-1))
    u_turn = lon_pad(jnp.roll(u_wind, -half_lon, axis=-1))
    v_turn = lon_pad(jnp.roll(v_wind, -half_lon, axis=-1))
    h_ext = jnp.concatenate([h_turn[:, :1], h_pad, h_turn[:, -1:]], 1)
    u_ext = jnp.concatenate([-u_turn[:, :1], u_pad, -u_turn[:, -1:]], 1)
    v_ext = jnp.concatenate([jnp.zeros_like(v_pad[:, :1]), v_pad, -v_turn[:, -2:-1]], 1)
    stepped = stencil(jnp.stack([h_ext, u_ext, v_ext]), 0, NLAT)
    height_next = polar_filter(stepped[0])
    u_next = polar_filter(stepped[1])
    v_next = polar_filter(stepped[2])
    return jnp.swapaxes(u_next, 1, 2), jnp.swapaxes(v_next, 1, 2), jnp.swapaxes(height_next, 1, 2)
```

```python
import functools
import math

import jax
import jax.numpy as jnp
import numpy as np
from jax import lax
from jax.experimental import pallas as pl
from jax.experimental.pallas import tpu as pltpu
from jax.sharding import PartitionSpec as P

N_LON = 16
N_LAT = 8
LEV = 16
COLS = 180
ROWS = 128
NLON = N_LON * COLS
NLAT = N_LAT * ROWS
HALF = 192
TOP = 8
TALL = 200
STEP = 4
AXES = ("lon", "lat")

GRAV_ZONAL = 0.3
GRAV_MERID = 0.6
CORIOLIS = 0.8
DIVERGENCE = 0.3
DIFFUSION = 0.08


def latitude_tables():
    f32 = np.float32
    index = np.arange(NLAT).astype(f32)
    step = f32(math.pi / NLAT)

    def sine(angle):
        return np.sin(angle.astype(np.float64)).astype(f32)

    def cosine(angle):
        return np.cos(angle.astype(np.float64)).astype(f32)

    center = (index + f32(0.5)) * step
    face = (index + f32(1.0)) * step
    cos_center = sine(center)
    sin_center = -cosine(center)
    sin_face = -cosine(face)
    cos_face = np.where(index + 1 < NLAT, sine(face), f32(0.0))
    cos_south = sine(index * step)
    ratio = f32(2.0) * cos_center * cos_center
    table = np.stack(
        [
            GRAV_ZONAL / cos_center.astype(np.float64),
            CORIOLIS * 0.25 * sin_center.astype(np.float64),
            CORIOLIS * 0.25 * sin_face.astype(np.float64),
            cos_face,
            cos_south,
            ratio,
            DIVERGENCE / cos_center.astype(np.float64),
            np.zeros(NLAT),
        ]
    ).astype(f32)
    return np.ascontiguousarray(table.reshape(8, N_LAT, ROWS).transpose(1, 0, 2))


def split(value):
    high = value.astype(jnp.bfloat16)
    return high, (value - high.astype(value.dtype)).astype(jnp.bfloat16)


@functools.cache
def fourier_tables():
    forward = np.zeros((8, 2 * HALF, 2 * HALF))
    inverse = np.zeros((8, 2 * HALF, 2 * HALF))
    wave = np.zeros((8, 2 * HALF), np.int64)
    m = np.arange(COLS)
    first = slice(0, COLS)
    second = slice(HALF, HALF + COLS)

    def angle(k):
        return (k[:, None] * m[None, :] % NLON) * (2.0 * math.pi / NLON)

    for q in range(1, 8):
        k = q + 16 * np.arange(COLS)
        cos, sin = np.cos(angle(k)), np.sin(angle(k))
        forward[q, first, first] = cos
        forward[q, first, second] = sin
        forward[q, second, first] = -sin
        forward[q, second, second] = cos
        wave[q, first] = wave[q, second] = k
        inverse[q] = forward[q].T * (2.0 / NLON)
    k_cos, k_sin = 16 * np.arange(91), 16 * np.arange(1, 90)
    forward[0, first, first] = np.concatenate([np.cos(angle(k_cos)), np.sin(angle(k_sin))])
    wave[0, first] = np.concatenate([k_cos, k_sin])
    k_both = 8 + 16 * np.arange(90)
    forward[0, second, second] = np.concatenate([np.cos(angle(k_both)), np.sin(angle(k_both))])
    wave[0, second] = np.concatenate([k_both, k_both])
    weight = np.where((wave[0] == 0) | (wave[0] == NLON // 2), 1.0, 2.0) / NLON
    inverse[0] = (forward[0] * weight[:, None]).T
    wave = np.minimum(wave, NLON - wave)
    sine = np.sin((wave.astype(np.float32) * np.float32(math.pi / NLON)).astype(np.float64))
    sine_sq = (sine.astype(np.float32) * sine.astype(np.float32)).astype(np.float64)
    over = np.where(wave == 0, 1e30, 1.0 / np.where(wave == 0, 1.0, sine_sq)).astype(np.float32)

    def halves(matrix):
        matrix = matrix.astype(np.float32)
        high = matrix.astype(jnp.bfloat16)
        low = (matrix - high.astype(np.float32)).astype(jnp.bfloat16)
        return np.concatenate([high, low], axis=1)

    over = np.ascontiguousarray(np.broadcast_to(over[:, :, None], (8, 2 * HALF, ROWS)))
    return halves(forward), halves(inverse), over


SIN = [math.sin(math.pi * t / 8) for t in range(5)]


def times(value, c, s):
    re, im = value
    return (c * re - s * im, c * im + s * re)


def forward16(x):
    e = [x[p] + x[p + 8] for p in range(8)]
    o = [x[p] - x[p + 8] for p in range(8)]
    e2 = [e[p] + e[p + 4] for p in range(4)]
    o2 = [e[p] - e[p + 4] for p in range(4)]
    a, b = e2[0] + e2[2], e2[1] + e2[3]
    pairs = [None] * 8
    pairs[0] = (a + b, a - b)
    pairs[4] = (e2[0] - e2[2], e2[3] - e2[1])
    root = SIN[2]
    u = (o2[0], -o2[2])
    w = times((o2[1], -o2[3]), root, -root)
    pairs[2] = (u[0] + w[0], u[1] + w[1])
    pairs[6] = (u[0] - w[0], w[1] - u[1])
    d = [times((o[p], -o[p + 4]), SIN[4 - p], -SIN[p]) if p else (o[p], -o[p + 4]) for p in range(4)]
    s02 = (d[0][0] + d[2][0], d[0][1] + d[2][1])
    t02 = (d[0][0] - d[2][0], d[0][1] - d[2][1])
    s13 = (d[1][0] + d[3][0], d[1][1] + d[3][1])
    t13 = (d[1][0] - d[3][0], d[1][1] - d[3][1])
    pairs[1] = (s02[0] + s13[0], s02[1] + s13[1])
    pairs[7] = (s02[0] - s13[0], s13[1] - s02[1])
    pairs[5] = (t02[0] + t13[1], t02[1] - t13[0])
    pairs[3] = (t02[0] - t13[1], -(t02[1] + t13[0]))
    return pairs


def inverse16(pairs):
    z0, z8 = pairs[0]
    a, b = z0 + z8, z0 - z8
    e2 = [a + pairs[4][0], b - pairs[4][1], a - pairs[4][0], b + pairs[4][1]]
    u, v = pairs[2], (pairs[6][0], -pairs[6][1])
    d0 = (u[0] + v[0], u[1] + v[1])
    root = SIN[2]
    d1 = times((u[0] - v[0], u[1] - v[1]), root, root)
    o2 = [d0[0], d1[0], -d0[1], -d1[1]]
    e = [e2[p] + o2[p] for p in range(4)] + [e2[p] - o2[p] for p in range(4)]
    a1, a5 = pairs[1], pairs[5]
    a9, a13 = (pairs[7][0], -pairs[7][1]), (pairs[3][0], -pairs[3][1])
    s19 = (a1[0] + a9[0], a1[1] + a9[1])
    t19 = (a1[0] - a9[0], a1[1] - a9[1])
    s5 = (a5[0] + a13[0], a5[1] + a13[1])
    t5 = (a5[0] - a13[0], a5[1] - a13[1])
    d = [
        (s19[0] + s5[0], s19[1] + s5[1]),
        (t19[0] - t5[1], t19[1] + t5[0]),
        (s19[0] - s5[0], s19[1] - s5[1]),
        (t19[0] + t5[1], t19[1] - t5[0]),
    ]
    d = [times(d[p], SIN[4 - p], SIN[p]) if p else d[p] for p in range(4)]
    o = [d[p][0] for p in range(4)] + [-d[p][1] for p in range(4)]
    return [e[p] + o[p] for p in range(8)] + [e[p] - o[p] for p in range(8)]


def pack_kernel(h, u, v, west, east, low, high):
    step = pl.program_id(0)

    @pl.when(step == 0)
    def _():
        low[...] = jnp.zeros_like(low)
        high[...] = jnp.zeros_like(high)

    parts = (
        (pl.ds(TOP, COLS), lambda field, f, i, level: field[i]),
        (pl.ds(TOP - 1, 1), lambda field, f, i, level: west[f, pl.ds(level, 1), :]),
        (pl.ds(TOP + COLS, 1), lambda field, f, i, level: east[f, pl.ds(level, 1), :]),
    )
    for rows, read in parts:
        south, north = low[rows, :], high[rows, :]
        lane = lax.broadcasted_iota(jnp.int32, south.shape, 1)
        for i in range(STEP):
            level = step * STEP + i
            for f, field in enumerate((h, u, v)):
                block = read(field, f, i, level)
                spot = 16 * f + level
                south = jnp.where(lane == spot, pltpu.roll(block, spot, 1), south)
                north = jnp.where(lane == spot, pltpu.roll(block, spot + 1, 1), north)
                if f == 2:
                    north = jnp.where(
                        lane == spot + 16, pltpu.roll(block, spot + 18, 1), north
                    )
        low[rows, :] = south
        high[rows, :] = north


def pack(height, u_wind, v_wind, west, east):
    field = pl.BlockSpec((STEP, COLS, ROWS), lambda i: (i, 0, 0))
    side = pl.BlockSpec((3, LEV, ROWS), lambda i: (0, 0, 0))
    edge = pl.BlockSpec((TALL, ROWS), lambda i: (0, 0))
    shape = jax.ShapeDtypeStruct((TALL, ROWS), jnp.float32)
    return pl.pallas_call(
        pack_kernel,
        grid=(LEV // STEP,),
        in_specs=[field, field, field, side, side],
        out_specs=[edge, edge],
        out_shape=[shape, shape],
        cost_estimate=pl.CostEstimate(flops=0, bytes_accessed=4_700_000, transcendentals=0),
    )(height, u_wind, v_wind, west, east)


def stencil_kernel(
    place, h, u, v, west, east, above, below, across, table, uv_out, h_out, e, rim, t_sum, w_sum
):
    step = pl.program_id(0)
    at_north, at_south = place[1] == 1, place[2] == 1
    lane = lax.broadcasted_iota(jnp.int32, (TALL, ROWS), 1)

    @pl.when(step == 0)
    def _():
        turned = across[...]
        rim[0] = jnp.where(at_north, jnp.where(lane < 16, turned, -turned), above[...])
        south = jnp.where(lane < 16, turned, jnp.where(lane < 32, -turned, 0.0))
        rim[1] = jnp.where(at_south, south, below[...])

    zonal, turn_u, turn_v, cos_face, cos_south, _, diverge = (
        table[0, i : i + 1, :] for i in range(7)
    )
    here, to_west, to_east = (pl.ds(TOP + i, 184) for i in (0, -1, 1))
    inner = slice(TOP, TOP + 184)

    def diffuse(f, middle, north, south):
        around = e[f, to_east, :] + e[f, to_west, :] + north[inner] + south[inner]
        return DIFFUSION * (around - 4.0 * middle)

    for i in range(h.shape[0]):
        level = step * h.shape[0] + i
        north, south = [], []
        for f, field in enumerate((h, u, v)):
            e[f, pl.ds(TOP, COLS), :] = field[i]
            e[f, pl.ds(TOP - 1, 1), :] = west[f, pl.ds(level, 1), :]
            e[f, pl.ds(TOP + COLS, 1), :] = east[f, pl.ds(level, 1), :]
            block = e[f]
            spot = 16 * f + level
            spot_north = jnp.where(at_north, spot + 16, spot) if f == 2 else spot
            edge = pltpu.roll(rim[0], ROWS - 1 - spot_north, 1)
            north.append(jnp.where(lane == ROWS - 1, edge, pltpu.roll(block, ROWS - 1, 1)))
            edge = pltpu.roll(rim[1], lax.rem(ROWS - spot, ROWS), 1)
            south.append(jnp.where(lane == 0, edge, pltpu.roll(block, 1, 1)))
        t_sum[...] = e[1] + north[1]
        w_sum[...] = e[2] + south[2]
        mid_h, mid_u, mid_v = (e[f, here, :] for f in range(3))
        new_u = (
            mid_u
            - zonal * (e[0, to_east, :] - mid_h)
            + turn_u * (w_sum[here, :] + w_sum[to_east, :])
            + diffuse(1, mid_u, north[1], south[1])
        )
        new_v = (
            mid_v
            - GRAV_MERID * (north[0][inner] - mid_h)
            - turn_v * (t_sum[here, :] + t_sum[to_west, :])
            + diffuse(2, mid_v, north[2], south[2])
        )
        flux = mid_u - e[1, to_west, :] + cos_face * mid_v - cos_south * south[2][inner]
        new_h = mid_h - diverge * flux + diffuse(0, mid_h, north[0], south[0])
        uv_out[i, 0] = new_u[:COLS]
        uv_out[i, 1] = new_v[:COLS]
        h_out[i] = new_h[:COLS]


def stencil(place, height, u_wind, v_wind, west, east, above, below, across, tables):
    some = 2
    field = pl.BlockSpec((some, COLS, ROWS), lambda i, s: (i, 0, 0))
    side = pl.BlockSpec((3, LEV, ROWS), lambda i, s: (0, 0, 0))
    edge = pl.BlockSpec((TALL, ROWS), lambda i, s: (0, 0))
    table = pl.BlockSpec((1, 8, ROWS), lambda i, s: (s[0], 0, 0))
    pair = pl.BlockSpec((some, 2, COLS, ROWS), lambda i, s: (i, 0, 0, 0))
    tall = pltpu.VMEM((TALL, ROWS), jnp.float32)
    return pl.pallas_call(
        stencil_kernel,
        grid_spec=pltpu.PrefetchScalarGridSpec(
            num_scalar_prefetch=1,
            grid=(LEV // some,),
            in_specs=[field, field, field, side, side, edge, edge, edge, table],
            out_specs=[pair, field],
            scratch_shapes=[
                pltpu.VMEM((3, TALL, ROWS), jnp.float32),
                pltpu.VMEM((2, TALL, ROWS), jnp.float32),
                tall,
                tall,
            ],
        ),
        out_shape=[
            jax.ShapeDtypeStruct((LEV, 2, COLS, ROWS), jnp.float32),
            jax.ShapeDtypeStruct((LEV, COLS, ROWS), jnp.float32),
        ],
        cost_estimate=pl.CostEstimate(
            flops=50_000_000, bytes_accessed=9_000_000, transcendentals=0
        ),
    )(place, height, u_wind, v_wind, west, east, above, below, across, tables)


def filter_kernel(items, place, x, forward, inverse, over, table, out, spectra, waves):
    q = pl.program_id(0)
    full = COLS // 16
    rest = COLS - 16 * full

    @pl.when(q == 0)
    def _():
        def gather(start, item, read):
            lanes = slice(item * ROWS, (item + 1) * ROWS)
            pairs = forward16([read(p) for p in range(16)])
            for part in range(8):
                for side in range(2):
                    rows = pl.ds(pl.multiple_of(side * HALF + start, 16), 16)
                    high, low = split(pairs[part][side])
                    spectra[part, 0, rows, lanes] = high
                    spectra[part, 1, rows, lanes] = low

        for item in range(items):

            def chunk(c, carry, item=item):
                start = pl.multiple_of(c * 16, 16)
                gather(start, item, lambda p: x[p, item, pl.ds(start, 16), :])
                return carry

            lax.fori_loop(0, full, chunk, 0)
            empty = jnp.zeros((16 - rest, ROWS), jnp.float32)
            gather(
                16 * full,
                item,
                lambda p, item=item: jnp.concatenate(
                    [x[p, item, pl.ds(16 * full, rest), :], empty], 0
                ),
            )

    def product(matrix, high, low):
        both = jnp.dot(matrix[0], high, preferred_element_type=jnp.float32)
        small = jnp.dot(matrix[0, : 2 * HALF], low, preferred_element_type=jnp.float32)
        return both[: 2 * HALF] + (both[2 * HALF :] + small)

    found = product(forward, spectra[q, 0], spectra[q, 1])
    damping = jnp.minimum(table[0, 5:6, :] * over[0], 1.0)
    damped = jnp.concatenate(
        [found[:, i * ROWS : (i + 1) * ROWS] * damping for i in range(items)], 1
    )
    waves[q] = product(inverse, *split(damped))

    @pl.when(q == 7)
    def _():
        def scatter(start, item, count):
            lanes = slice(item * ROWS, (item + 1) * ROWS)
            pairs = [
                tuple(
                    waves[part, pl.ds(pl.multiple_of(side * HALF + start, 8), 8), lanes]
                    for side in range(2)
                )
                for part in range(8)
            ]
            for p, value in enumerate(inverse16(pairs)):
                out[p, item, pl.ds(start, count), :] = value[:count]

        for item in range(items):

            def chunk(c, carry, item=item):
                scatter(pl.multiple_of(c * 8, 8), item, 8)
                return carry

            lax.fori_loop(0, COLS // 8, chunk, 0)
            scatter(8 * (COLS // 8), item, COLS % 8)


def polar_filter(place, x, tables):
    items = x.shape[1]
    forward, inverse, over = fourier_tables()
    wide = items * ROWS
    whole = pl.BlockSpec(x.shape, lambda q, s: (0, 0, 0, 0), pipeline_mode=pl.Buffered(1))
    matrix = pl.BlockSpec((1, 4 * HALF, 2 * HALF), lambda q, s: (q, 0, 0))
    return pl.pallas_call(
        functools.partial(filter_kernel, items),
        grid_spec=pltpu.PrefetchScalarGridSpec(
            num_scalar_prefetch=1,
            grid=(8,),
            in_specs=[
                whole,
                matrix,
                matrix,
                pl.BlockSpec((1, 2 * HALF, ROWS), lambda q, s: (q, 0, 0)),
                pl.BlockSpec((1, 8, ROWS), lambda q, s: (s[0], 0, 0)),
            ],
            out_specs=pl.BlockSpec(x.shape, lambda q, s: (0, 0, 0, 0)),
            scratch_shapes=[
                pltpu.VMEM((8, 2, 2 * HALF, wide), jnp.bfloat16),
                pltpu.VMEM((8, 2 * HALF, wide), jnp.float32),
            ],
        ),
        out_shape=jax.ShapeDtypeStruct(x.shape, jnp.float32),
        compiler_params=pltpu.CompilerParams(vmem_limit_bytes=56 * 1024 * 1024),
        cost_estimate=pl.CostEstimate(
            flops=96 * (2 * HALF) ** 2 * wide, bytes_accessed=15_000_000, transcendentals=0
        ),
    )(place, x, jnp.asarray(forward), jnp.asarray(inverse), jnp.asarray(over), tables)


def around(lat, shift, distance):
    return [
        (lon * N_LAT + lat, (lon + distance) % N_LON * N_LAT + (lat + shift))
        for lon in range(N_LON)
    ]


def shards(u_wind, v_wind, height):
    band = lax.axis_index("lat")
    at_north, at_south = band == N_LAT - 1, band == 0
    place = jnp.stack([band, at_north, at_south]).astype(jnp.int32)
    tables = jnp.asarray(latitude_tables())
    fields = (height, u_wind, v_wind)
    last = jnp.stack([field[:, COLS - 1, :] for field in fields])
    initial = jnp.stack([field[:, 0, :] for field in fields])
    east_to = [(i, (i + 1) % N_LON) for i in range(N_LON)]
    west = lax.ppermute(last, "lon", east_to)
    east = lax.ppermute(initial, "lon", [(j, i) for i, j in east_to])
    low, high = pack(height, u_wind, v_wind, west, east)
    below = lax.ppermute(high, "lat", [(i, i + 1) for i in range(N_LAT - 1)])
    above = lax.ppermute(low, "lat", [(i + 1, i) for i in range(N_LAT - 1)])
    across = lax.ppermute(
        jnp.where(at_north, high, low),
        AXES,
        around(0, 0, N_LON // 2) + around(N_LAT - 1, 0, N_LON // 2),
    )
    uv, h = stencil(place, height, u_wind, v_wind, west, east, above, below, across, tables)

    def exchange(value):
        return lax.all_to_all(value, "lon", split_axis=0, concat_axis=0, tiled=True)

    def smooth(value):
        return exchange(polar_filter(place, exchange(value), tables))

    def filtered(uv, h):
        whole = jnp.concatenate([uv, h[:, None]], 1)
        result = smooth(whole)
        return result[:, 0], result[:, 1], result[:, 2]

    is_polar = (band < N_LAT // 4) | (band >= N_LAT - N_LAT // 4)
    return lax.cond(is_polar, filtered, lambda uv, h: (uv[:, 0], uv[:, 1], h), uv, h)


def solution(mesh):
    placed = (P(None, "lon", "lat"),) * 3
    return jax.shard_map(shards, mesh=mesh, in_specs=placed, out_specs=placed, check_vma=False)
```

```python
import functools
import math

import jax
import jax.numpy as jnp
import numpy as np
from jax import lax
from jax.experimental import pallas as pl
from jax.experimental.pallas import tpu as pltpu
from jax.sharding import PartitionSpec as P

N_LON = 16
N_LAT = 8
LEV = 16
COLS = 180
ROWS = 128
NLON = N_LON * COLS
NLAT = N_LAT * ROWS
HALF = 192
TALL = 184
PACK = 90
CHUNK = 48
SOME = 96
AHEAD = 16
AXES = ("lon", "lat")

GRAV_ZONAL = 0.3
GRAV_MERID = 0.6
CORIOLIS = 0.8
DIVERGENCE = 0.3
DIFFUSION = 0.08


def latitude_tables():
    f32 = np.float32
    index = np.arange(NLAT).astype(f32)
    step = f32(math.pi / NLAT)

    def sine(angle):
        return np.sin(angle.astype(np.float64)).astype(f32)

    def cosine(angle):
        return np.cos(angle.astype(np.float64)).astype(f32)

    center = (index + f32(0.5)) * step
    face = (index + f32(1.0)) * step
    cos_center = sine(center)
    sin_center = -cosine(center)
    sin_face = -cosine(face)
    cos_face = np.where(index + 1 < NLAT, sine(face), f32(0.0))
    cos_south = sine(index * step)
    ratio = f32(2.0) * cos_center * cos_center
    table = np.stack(
        [
            GRAV_ZONAL / cos_center.astype(np.float64),
            CORIOLIS * 0.25 * sin_center.astype(np.float64),
            CORIOLIS * 0.25 * sin_face.astype(np.float64),
            cos_face,
            cos_south,
            ratio,
            DIVERGENCE / cos_center.astype(np.float64),
            np.zeros(NLAT),
        ]
    ).astype(f32)
    return np.ascontiguousarray(table.reshape(8, N_LAT, ROWS).transpose(1, 0, 2))


def split(value):
    high = value.astype(jnp.bfloat16)
    return high, (value - high.astype(value.dtype)).astype(jnp.bfloat16)


@functools.cache
def fourier_tables():
    at = np.arange(COLS)
    angles = (at[:, None] * at[None, :] % COLS) * (2.0 * math.pi / COLS)
    matrix = np.zeros((2, HALF, HALF), np.float32)
    matrix[0, :COLS, :COLS] = np.cos(angles)
    matrix[1, :COLS, :COLS] = np.sin(angles)
    matrix = matrix.reshape(2 * HALF, HALF)
    high = matrix.astype(jnp.bfloat16)
    low = (matrix - high.astype(np.float32)).astype(jnp.bfloat16)
    columns = np.zeros((HALF, ROWS), np.float32)
    for q in range(9):
        turn = q * at * (2.0 * math.pi / NLON)
        columns[:COLS, q] = np.cos(turn)
        columns[:COLS, 16 + q] = -np.sin(turn)
        wave = q + 16 * at
        wave = np.minimum(wave, NLON - wave)
        sine = np.sin((wave.astype(np.float32) * np.float32(math.pi / NLON)).astype(np.float64))
        sine_sq = (sine.astype(np.float32) * sine.astype(np.float32)).astype(np.float64)
        over = np.where(wave == 0, 1e30, 1.0 / np.where(wave == 0, 1.0, sine_sq))
        columns[:COLS, 32 + q] = over * scale_of(q)
    return np.concatenate([high, low], axis=0), columns


def scale_of(q):
    return (1.0 if q in (0, 8) else 2.0) / NLON


SIN = [math.sin(math.pi * t / 8) for t in range(5)]


def times(value, c, s):
    re, im = value
    return (c * re - s * im, c * im + s * re)


def forward16(x):
    e = [x[p] + x[p + 8] for p in range(8)]
    o = [x[p] - x[p + 8] for p in range(8)]
    e2 = [e[p] + e[p + 4] for p in range(4)]
    o2 = [e[p] - e[p + 4] for p in range(4)]
    a, b = e2[0] + e2[2], e2[1] + e2[3]
    pairs = [None] * 8
    pairs[0] = (a + b, a - b)
    pairs[4] = (e2[0] - e2[2], e2[3] - e2[1])
    root = SIN[2]
    u = (o2[0], -o2[2])
    w = times((o2[1], -o2[3]), root, -root)
    pairs[2] = (u[0] + w[0], u[1] + w[1])
    pairs[6] = (u[0] - w[0], w[1] - u[1])
    d = [times((o[p], -o[p + 4]), SIN[4 - p], -SIN[p]) if p else (o[p], -o[p + 4]) for p in range(4)]
    s02 = (d[0][0] + d[2][0], d[0][1] + d[2][1])
    t02 = (d[0][0] - d[2][0], d[0][1] - d[2][1])
    s13 = (d[1][0] + d[3][0], d[1][1] + d[3][1])
    t13 = (d[1][0] - d[3][0], d[1][1] - d[3][1])
    pairs[1] = (s02[0] + s13[0], s02[1] + s13[1])
    pairs[7] = (s02[0] - s13[0], s13[1] - s02[1])
    pairs[5] = (t02[0] + t13[1], t02[1] - t13[0])
    pairs[3] = (t02[0] - t13[1], -(t02[1] + t13[0]))
    return pairs


def inverse16(pairs):
    z0, z8 = pairs[0]
    a, b = z0 + z8, z0 - z8
    e2 = [a + pairs[4][0], b - pairs[4][1], a - pairs[4][0], b + pairs[4][1]]
    u, v = pairs[2], (pairs[6][0], -pairs[6][1])
    d0 = (u[0] + v[0], u[1] + v[1])
    root = SIN[2]
    d1 = times((u[0] - v[0], u[1] - v[1]), root, root)
    o2 = [d0[0], d1[0], -d0[1], -d1[1]]
    e = [e2[p] + o2[p] for p in range(4)] + [e2[p] - o2[p] for p in range(4)]
    a1, a5 = pairs[1], pairs[5]
    a9, a13 = (pairs[7][0], -pairs[7][1]), (pairs[3][0], -pairs[3][1])
    s19 = (a1[0] + a9[0], a1[1] + a9[1])
    t19 = (a1[0] - a9[0], a1[1] - a9[1])
    s5 = (a5[0] + a13[0], a5[1] + a13[1])
    t5 = (a5[0] - a13[0], a5[1] - a13[1])
    d = [
        (s19[0] + s5[0], s19[1] + s5[1]),
        (t19[0] - t5[1], t19[1] + t5[0]),
        (s19[0] - s5[0], s19[1] - s5[1]),
        (t19[0] + t5[1], t19[1] - t5[0]),
    ]
    d = [times(d[p], SIN[4 - p], SIN[p]) if p else d[p] for p in range(4)]
    o = [d[p][0] for p in range(4)] + [-d[p][1] for p in range(4)]
    return [e[p] + o[p] for p in range(8)] + [e[p] - o[p] for p in range(8)]


def row(i):
    return pl.ds(pl.multiple_of(i * LEV, LEV), LEV)


def lanes_of(shape):
    return lax.broadcasted_iota(jnp.int32, shape, len(shape) - 1)


def pack_kernel(place, h, u, v, first, second, low, high):
    step = pl.program_id(0)

    @pl.when(step == 0)
    def _():
        low[...] = jnp.zeros_like(low)
        high[...] = jnp.zeros_like(high)

    spots = [lanes_of((LEV, ROWS)) + ROWS * part for part in range(2)]
    kept_low = [[low[f, part] for part in range(2)] for f in range(3)]
    kept_high = [[high[f, part] for part in range(2)] for f in range(4)]
    for i in range(PACK):
        spot = step * PACK + i + 1
        masks = [[s == spot + k for s in spots] for k in (-1, 0, 1)]
        for f, field in enumerate((h, u, v)):
            turned = pltpu.roll(field[i * LEV : (i + 1) * LEV, :], lax.rem(spot + 1, ROWS), 1)
            for part in range(2):
                kept_high[f][part] = jnp.where(masks[1][part], turned, kept_high[f][part])
                kept_low[f][part] = jnp.where(masks[2][part], turned, kept_low[f][part])
                if f == 2:
                    kept_high[3][part] = jnp.where(masks[0][part], turned, kept_high[3][part])
    for part in range(2):
        for f in range(3):
            low[f, part] = kept_low[f][part]
        for f in range(4):
            high[f, part] = kept_high[f][part]

    @pl.when(step == pl.num_programs(0) - 1)
    def _():
        even = place[4] == 1
        for f in range(4):
            if f < 3:
                south = shift_lanes([low[f, 0], low[f, 1]], -1)
                north = [high[f, 0], high[f, 1]]
            else:
                south = [jnp.zeros((LEV, ROWS), jnp.float32)] * 2
                north = shift_lanes([high[f, 0], high[f, 1]], 1)
            for part in range(2):
                first[f, part] = jnp.where(even, north[part], south[part])
                second[f, part] = jnp.where(even, south[part], north[part])


def shift_lanes(parts, by):
    turned = [pltpu.roll(part, by % ROWS, 1) for part in parts]
    lane = lanes_of(parts[0].shape)
    fresh = lane == (0 if by > 0 else ROWS - 1)
    return [jnp.where(fresh, turned[1 - i], turned[i]) for i in range(2)]


def pack(place, height, u_wind, v_wind):
    field = pl.BlockSpec((PACK * LEV, ROWS), lambda i, s: (i, 0))
    shape = (4, 2, LEV, ROWS)
    edge = pl.BlockSpec(shape, lambda i, s: (0, 0, 0, 0))
    return pl.pallas_call(
        pack_kernel,
        grid_spec=pltpu.PrefetchScalarGridSpec(
            num_scalar_prefetch=1,
            grid=(COLS // PACK,),
            in_specs=[field, field, field],
            out_specs=[edge, edge],
            scratch_shapes=[pltpu.VMEM(shape, jnp.float32)] * 2,
        ),
        out_shape=[jax.ShapeDtypeStruct(shape, jnp.float32)] * 2,
        cost_estimate=pl.CostEstimate(flops=0, bytes_accessed=4_700_000, transcendentals=0),
    )(place, height, u_wind, v_wind)


def rim_terms(place, first, second, table, terms):
    even, at_north, at_south = place[4] == 1, place[1] == 1, place[2] == 1
    lane = lanes_of((LEV, ROWS))

    def rim(f, part):
        above = jnp.where(even, first[f, part], second[f, part])
        below = jnp.where(even, second[f, part], first[f, part])
        if f == 0:
            return above, below
        turned = -second[3 if f == 2 else f, part]
        across = -second[f, part] if f == 1 else jnp.zeros_like(below)
        return jnp.where(at_north, turned, above), jnp.where(at_south, across, below)

    (h_n, h_s), (u_n, u_s), (v_n, v_s) = (
        zip(*(rim(f, part) for part in range(2))) for f in range(3)
    )
    turn_u, cos_south, diverge = (table[0, i : i + 1, 0:1] for i in (1, 4, 6))
    turn_v = table[0, 2:3, ROWS - 1 : ROWS]
    u_nw, v_se = shift_lanes(u_n, 1), shift_lanes(v_s, -1)
    for part in range(2):
        north = (
            DIFFUSION * h_n[part],
            DIFFUSION * u_n[part],
            DIFFUSION * v_n[part] - GRAV_MERID * h_n[part] - turn_v * (u_n[part] + u_nw[part]),
        )
        south = (
            DIFFUSION * h_s[part] + diverge * cos_south * v_s[part],
            DIFFUSION * u_s[part] + turn_u * (v_s[part] + v_se[part]),
            DIFFUSION * v_s[part],
        )
        for f in range(3):
            after = pltpu.roll(south[f], 1, 1)
            for odd in range(2):
                terms[f, odd, part] = jnp.where(lane % 2 == odd, north[f], after)


def stencil_kernel(
    place, h, u, v, h_west, u_west, v_west, h_east, u_east, v_east, west, east, first, second, table,
    u_out, v_out, h_first, h_second, own_h, own_u, own_v, terms, whole,
):
    step = pl.program_id(0)
    lane = lanes_of((LEV, ROWS))
    edges = (lane == 0) | (lane == ROWS - 1)

    @pl.when(step == 0)
    def _():
        rim_terms(place, first, second, table, terms)

    zonal, turn_u, turn_v, cos_face, cos_south, _, diverge = (
        jnp.broadcast_to(table[0, i : i + 1, :], (LEV, ROWS)) for i in range(7)
    )

    def north(block):
        return jnp.where(lane == ROWS - 1, 0.0, pltpu.roll(block, ROWS - 1, 1))

    def south(block):
        return jnp.where(lane == 0, 0.0, pltpu.roll(block, 1, 1))

    def update(k, odd, carry, blocks_east):
        (t_west, v_south, w_here), (west_h, west_u, west_v) = carry
        mid_h, mid_u, mid_v = middle = [field[row(k), :] for field in (h, u, v)]
        east_h, east_u, east_v = blocks_east
        h_north, h_south = north(mid_h), south(mid_h)
        u_north, u_south = north(mid_u), south(mid_u)
        v_north, v_south_east = north(mid_v), south(east_v)
        t_here = mid_u + u_north
        w_east = east_v + v_south_east
        new_u = (
            mid_u
            - zonal * (east_h - mid_h)
            + turn_u * (w_here + w_east)
            + DIFFUSION * (east_u + west_u + (u_north + u_south) - 4.0 * mid_u)
        )
        new_v = (
            mid_v
            - GRAV_MERID * (h_north - mid_h)
            - turn_v * (t_here + t_west)
            + DIFFUSION * (east_v + west_v + (v_north + v_south) - 4.0 * mid_v)
        )
        new_h = (
            mid_h
            - diverge * (mid_u - west_u + cos_face * mid_v - cos_south * v_south)
            + DIFFUSION * (east_h + west_h + (h_north + h_south) - 4.0 * mid_h)
        )
        spot = step * CHUNK + k + 1
        turn = lax.rem(2 * ROWS - 1 - spot, ROWS)
        results = []
        for f, new in enumerate((new_h, new_u, new_v)):
            term = pltpu.roll(terms[f, odd, spot // ROWS], turn, 1)
            results.append(new + jnp.where(edges, term, 0.0))
        return ((t_here, v_south_east, w_east), middle), results

    def several(base, carry, beyond):
        found = []
        for n in range(AHEAD):
            k = base + n
            if n == AHEAD - 1 and beyond is not None:
                blocks = beyond
            else:
                blocks = [field[row(k + 1), :] for field in (h, u, v)]
            if n == (COLS - 1) % AHEAD:
                is_last = step * CHUNK + k == COLS - 1
                blocks = [jnp.where(is_last, east[f], blocks[f]) for f in range(3)]
            carry, results = update(k, (n + 1) % 2, carry, blocks)
            found.append(results)
        for n, results in enumerate(found):
            for f in range(3):
                whole[f, row(base + n), :] = results[f]
        return carry

    before = [
        jnp.where(step == 0, west[f], field[...]) for f, field in enumerate((h_west, u_west, v_west))
    ]
    here_v = v[row(0), :]
    v_south = south(here_v)
    carry = ((before[1] + north(before[1]), v_south, here_v + v_south), before)
    groups = CHUNK // AHEAD
    carry = lax.fori_loop(
        0, groups - 1, lambda c, carry: several(c * AHEAD, carry, None), carry
    )
    several((groups - 1) * AHEAD, carry, [field[...] for field in (h_east, u_east, v_east)])

    @pl.when(place[3] == 0)
    def _():
        for f, out in enumerate((own_h, own_u, own_v)):
            out[...] = whole[f]

    @pl.when(place[3] == 1)
    def _():
        def turned(f):
            return jnp.transpose(whole[f].reshape(CHUNK, LEV, ROWS), (1, 0, 2))

        height = turned(0)
        h_first[...] = height[: LEV // 2]
        h_second[...] = height[LEV // 2 :]
        u_out[...] = turned(1)
        v_out[...] = turned(2)


def stencil(place, height, u_wind, v_wind, west, east, first, second, tables):
    block = pl.BlockSpec((CHUNK * LEV, ROWS), lambda i, s: (i, 0))
    one_west = pl.BlockSpec((LEV, ROWS), lambda i, s: (jnp.maximum(i * CHUNK - 1, 0), 0))
    one_east = pl.BlockSpec(
        (LEV, ROWS), lambda i, s: (jnp.minimum((i + 1) * CHUNK, COLS - 1), 0)
    )
    side = pl.BlockSpec((3, LEV, ROWS), lambda i, s: (0, 0, 0))
    edge = pl.BlockSpec((4, 2, LEV, ROWS), lambda i, s: (0, 0, 0, 0))
    kept = pl.BlockSpec((CHUNK * LEV, ROWS), lambda i, s: (jnp.where(s[3] == 0, i, 0), 0))

    def sent(levels):
        return pl.BlockSpec(
            (levels, CHUNK, ROWS), lambda i, s: (0, jnp.where(s[3] == 1, i, 0), 0)
        )

    own = jax.ShapeDtypeStruct((COLS * LEV, ROWS), jnp.float32)
    full = jax.ShapeDtypeStruct((LEV, TALL, ROWS), jnp.float32)
    half = jax.ShapeDtypeStruct((LEV // 2, TALL, ROWS), jnp.float32)
    fields = (height, u_wind, v_wind)
    return pl.pallas_call(
        stencil_kernel,
        grid_spec=pltpu.PrefetchScalarGridSpec(
            num_scalar_prefetch=1,
            grid=(pl.cdiv(COLS, CHUNK),),
            in_specs=[block] * 3
            + [one_west] * 3
            + [one_east] * 3
            + [side] * 2
            + [edge] * 2
            + [pl.BlockSpec((1, 8, ROWS), lambda i, s: (s[0], 0, 0))],
            out_specs=[sent(LEV), sent(LEV), sent(LEV // 2), sent(LEV // 2)] + [kept] * 3,
            scratch_shapes=[
                pltpu.VMEM((3, 2, 2, LEV, ROWS), jnp.float32),
                pltpu.VMEM((3, CHUNK * LEV, ROWS), jnp.float32),
            ],
        ),
        out_shape=[full, full, half, half, own, own, own],
        compiler_params=pltpu.CompilerParams(vmem_limit_bytes=58 * 1024 * 1024),
        cost_estimate=pl.CostEstimate(
            flops=60_000_000, bytes_accessed=9_000_000, transcendentals=0
        ),
    )(place, *fields, *fields, *fields, west, east, first, second, tables)


def unpack_kernel(place, own, *refs):
    parts, out = refs[:-1], refs[-1]

    @pl.when(place[3] == 1)
    def _():
        whole = jnp.concatenate([x[...] for x in parts], 0)
        out[...] = jnp.transpose(whole, (1, 0, 2)).reshape(SOME * LEV, ROWS)

    @pl.when(place[3] == 0)
    def _():
        out[...] = own[...]


def unpack(place, own, *parts):
    def pick(polar):
        return lambda i, s: jnp.where(s[3] == polar, i, 0)

    kept, used = pick(0), pick(1)
    return pl.pallas_call(
        unpack_kernel,
        grid_spec=pltpu.PrefetchScalarGridSpec(
            num_scalar_prefetch=1,
            grid=(pl.cdiv(COLS, SOME),),
            in_specs=[pl.BlockSpec((SOME * LEV, ROWS), lambda i, s: (kept(i, s), 0))]
            + [
                pl.BlockSpec((x.shape[0], SOME, ROWS), lambda i, s: (0, used(i, s), 0))
                for x in parts
            ],
            out_specs=pl.BlockSpec((SOME * LEV, ROWS), lambda i, s: (i, 0)),
        ),
        out_shape=jax.ShapeDtypeStruct((COLS * LEV, ROWS), jnp.float32),
        compiler_params=pltpu.CompilerParams(vmem_limit_bytes=58 * 1024 * 1024),
        cost_estimate=pl.CostEstimate(
            flops=0, bytes_accessed=8 * COLS * LEV * ROWS, transcendentals=0
        ),
    )(place, own, *parts)


def filter_kernel(place, x, matrix, columns, table, out, spectra, waves):
    def column(rows, q):
        return columns[rows, q : q + 1]

    def gather(start, blocks):
        rows = pl.ds(pl.multiple_of(start, 16), 16)
        pairs = forward16(blocks)
        parts = [(pairs[0][0], None)] + pairs[1:] + [(pairs[0][1], None)]
        for q, (re, im) in enumerate(parts):
            if q == 0:
                im = jnp.zeros_like(re)
            else:
                c, s = column(rows, q), column(rows, 16 + q)
                re, im = (c * re, s * re) if im is None else times((re, im), c, s)
            for side, value in enumerate((re, im)):
                high, low = split(value)
                spectra[q, 0, rows, side * ROWS : (side + 1) * ROWS] = high
                spectra[q, 1, rows, side * ROWS : (side + 1) * ROWS] = low

    def fill(c, carry):
        start = pl.multiple_of(c * 16, 16)
        gather(start, [x[p, pl.ds(start, 16), :] for p in range(16)])
        return carry

    full = COLS // 16
    lax.fori_loop(0, full, fill, 0)
    empty = jnp.zeros((HALF - COLS, ROWS), jnp.float32)
    tail = pl.ds(16 * full, COLS % 16)
    gather(16 * full, [jnp.concatenate([x[p, tail, :], empty], 0) for p in range(16)])

    def product(high, low):
        found = jnp.dot(matrix[: 2 * HALF], high, preferred_element_type=jnp.float32)
        found += jnp.dot(matrix[2 * HALF :], high, preferred_element_type=jnp.float32)
        found += jnp.dot(matrix[: 2 * HALF], low, preferred_element_type=jnp.float32)
        cos, sin = found[:HALF], found[HALF:]
        return cos[:, :ROWS], cos[:, ROWS:], sin[:, :ROWS], sin[:, ROWS:]

    ratio = table[0, 5:6, :]
    rows = slice(0, HALF)
    for q in range(9):
        cos_re, cos_im, sin_re, sin_im = product(spectra[q, 0], spectra[q, 1])
        damping = jnp.minimum(ratio * column(rows, 32 + q), scale_of(q))
        re, im = damping * (cos_re + sin_im), damping * (cos_im - sin_re)
        cos_re, cos_im, sin_re, sin_im = product(*split(jnp.concatenate([re, im], 1)))
        re = cos_re - sin_im
        if q:
            im = cos_im + sin_re
            c, s = column(rows, q), column(rows, 16 + q)
            if q < 8:
                waves[q, 1] = c * im - s * re
            re = c * re + s * im
        waves[q, 0] = re

    def give(c, carry):
        rows = pl.ds(pl.multiple_of(c * 8, 8), 8)
        pairs = [(waves[0, 0, rows, :], waves[8, 0, rows, :])]
        pairs += [(waves[q, 0, rows, :], waves[q, 1, rows, :]) for q in range(1, 8)]
        for p, value in enumerate(inverse16(pairs)):
            out[p, rows, :] = value
        return carry

    lax.fori_loop(0, TALL // 8, give, 0)


def polar_filter(place, x, tables):
    matrix, columns = fourier_tables()
    whole = pl.BlockSpec(x.shape, lambda i, s: (0, 0, 0))
    return pl.pallas_call(
        filter_kernel,
        grid_spec=pltpu.PrefetchScalarGridSpec(
            num_scalar_prefetch=1,
            grid=(1,),
            in_specs=[
                whole,
                pl.BlockSpec(matrix.shape, lambda i, s: (0, 0)),
                pl.BlockSpec(columns.shape, lambda i, s: (0, 0)),
                pl.BlockSpec((1, 8, ROWS), lambda i, s: (s[0], 0, 0)),
            ],
            out_specs=whole,
            scratch_shapes=[
                pltpu.VMEM((9, 2, HALF, 2 * ROWS), jnp.bfloat16),
                pltpu.VMEM((9, 2, HALF, ROWS), jnp.float32),
            ],
        ),
        out_shape=jax.ShapeDtypeStruct(x.shape, jnp.float32),
        compiler_params=pltpu.CompilerParams(vmem_limit_bytes=58 * 1024 * 1024),
        cost_estimate=pl.CostEstimate(
            flops=216 * HALF * HALF * ROWS, bytes_accessed=3_500_000, transcendentals=0
        ),
    )(place, x, jnp.asarray(matrix), jnp.asarray(columns), tables)


BESIDE = ((0, 3), (1, 2), (6, 5), (7, 4))
BEYOND = ((0, 4), (1, 5), (6, 2), (7, 3))


def lent(pairs, turn):
    return [
        (lon * N_LAT + polar, (lon ^ turn) * N_LAT + other)
        for lon in range(N_LON)
        for polar, other in pairs
    ]


def returned(pairs, turn):
    return [(j, i) for i, j in lent(pairs, turn)]


def partner(band, pairs):
    return sum(jnp.where(band == other, polar, 0) for polar, other in pairs).astype(jnp.int32)


def shards(u_wind, v_wind, height):
    band = lax.axis_index("lat")
    is_polar = (band < N_LAT // 4) | (band >= N_LAT - N_LAT // 4)
    even = band % 2 == 0
    place = jnp.stack([band, band == N_LAT - 1, band == 0, is_polar, even]).astype(jnp.int32)
    tables = jnp.asarray(latitude_tables())
    fields = [jnp.swapaxes(x, 0, 1) for x in (height, u_wind, v_wind)]
    flat = [x.reshape(COLS * LEV, ROWS) for x in fields]
    east_to = [(i, (i + 1) % N_LON) for i in range(N_LON)]
    west = lax.ppermute(jnp.stack([x[COLS - 1] for x in fields]), "lon", east_to)
    east = lax.ppermute(jnp.stack([x[0] for x in fields]), "lon", [(j, i) for i, j in east_to])
    first, second = pack(place, *flat)
    spot = lax.broadcasted_iota(jnp.int32, first.shape, 1) * ROWS + lax.broadcasted_iota(
        jnp.int32, first.shape, 3
    )

    def widened(value, is_north):
        def edge(side):
            north = [side[f, :, ROWS - 1 - (f == 3) :][:, :1] for f in range(3)]
            north.append(side[2, :, ROWS - 2 : ROWS - 1])
            south = [side[min(f, 2), :, :1] for f in range(4)]
            return jnp.where(is_north, jnp.stack(north), jnp.stack(south))[:, None]

        value = jnp.where(spot == 0, edge(west), value)
        return jnp.where(spot == COLS + 1, edge(east), value)

    swap = [(i, i ^ 1) for i in range(N_LAT)]
    first = lax.ppermute(widened(first, even), "lat", swap)
    routes = [(lon, i, lon, i + 1) for lon in range(N_LON) for i in range(1, N_LAT - 1, 2)]
    routes += [(lon, i + 1, lon, i) for lon, i, _, _ in routes]
    routes += [
        (lon, i, (lon + N_LON // 2) % N_LON, i) for lon in range(N_LON) for i in (0, N_LAT - 1)
    ]
    second = lax.ppermute(
        widened(second, jnp.logical_not(even)),
        AXES,
        [(a * N_LAT + b, c * N_LAT + d) for a, b, c, d in routes],
    )
    u, v, h_first, h_second, own_h, own_u, own_v = stencil(
        place, *flat, west, east, first, second, tables
    )

    def exchange(value):
        return lax.all_to_all(value, "lon", split_axis=0, concat_axis=0, tiled=True)

    def keep(u, v_circles, h_first, h_second):
        u_circles = exchange(u)
        v = exchange(polar_filter(place, v_circles, tables))
        return v, polar_filter(place, u_circles, tables)

    def help_out(u, v_circles, h_first, h_second):
        circles = exchange(jnp.concatenate([h_first, h_second], 0))
        lender = jnp.where(
            lax.axis_index("lon") < N_LON // 2, partner(band, BESIDE), partner(band, BEYOND)
        )
        smooth = polar_filter(lender.reshape(1), circles, tables)
        return exchange(smooth), smooth

    h_first = lax.ppermute(h_first, AXES, lent(BESIDE, 0))
    h_second = lax.ppermute(h_second, AXES, lent(BEYOND, N_LON // 2))
    v_circles = exchange(v)
    v_or_h, u = lax.cond(is_polar, keep, help_out, u, v_circles, h_first, h_second)
    h_first = lax.ppermute(v_or_h[: LEV // 2], AXES, returned(BESIDE, 0))
    h_second = lax.ppermute(v_or_h[LEV // 2 :], AXES, returned(BEYOND, N_LON // 2))
    u = exchange(u)
    result = (
        unpack(place, own_u, u),
        unpack(place, own_v, v_or_h),
        unpack(place, own_h, h_first, h_second),
    )
    return tuple(jnp.swapaxes(x.reshape(COLS, LEV, ROWS), 0, 1) for x in result)


def solution(mesh):
    placed = (P(None, "lon", "lat"),) * 3
    return jax.shard_map(shards, mesh=mesh, in_specs=placed, out_specs=placed, check_vma=False)
```

```python
import functools
import math

import jax
import jax.numpy as jnp
import numpy as np
from jax import lax
from jax.experimental import pallas as pl
from jax.experimental.pallas import tpu as pltpu
from jax.sharding import PartitionSpec as P

N_LON = 16
N_LAT = 8
LEV = 16
COLS = 180
ROWS = 128
NLON = N_LON * COLS
NLAT = N_LAT * ROWS
HALF = 192
TALL = 184
PACK = 90
CHUNK = 48
SOME = 96
AHEAD = 16
AXES = ("lon", "lat")

GRAV_ZONAL = 0.3
GRAV_MERID = 0.6
CORIOLIS = 0.8
DIVERGENCE = 0.3
DIFFUSION = 0.08


def latitude_tables():
    f32 = np.float32
    index = np.arange(NLAT).astype(f32)
    step = f32(math.pi / NLAT)

    def sine(angle):
        return np.sin(angle.astype(np.float64)).astype(f32)

    def cosine(angle):
        return np.cos(angle.astype(np.float64)).astype(f32)

    center = (index + f32(0.5)) * step
    face = (index + f32(1.0)) * step
    cos_center = sine(center)
    sin_center = -cosine(center)
    sin_face = -cosine(face)
    cos_face = np.where(index + 1 < NLAT, sine(face), f32(0.0))
    cos_south = sine(index * step)
    ratio = f32(2.0) * cos_center * cos_center
    table = np.stack(
        [
            GRAV_ZONAL / cos_center.astype(np.float64),
            CORIOLIS * 0.25 * sin_center.astype(np.float64),
            CORIOLIS * 0.25 * sin_face.astype(np.float64),
            cos_face,
            cos_south,
            ratio,
            DIVERGENCE / cos_center.astype(np.float64),
            np.zeros(NLAT),
        ]
    ).astype(f32)
    return np.ascontiguousarray(table.reshape(8, N_LAT, ROWS).transpose(1, 0, 2))


def split(value):
    high = value.astype(jnp.bfloat16)
    return high, (value - high.astype(value.dtype)).astype(jnp.bfloat16)


@functools.cache
def fourier_tables():
    at = np.arange(COLS)
    angles = (at[:, None] * at[None, :] % COLS) * (2.0 * math.pi / COLS)
    matrix = np.zeros((2, HALF, HALF), np.float32)
    matrix[0, :COLS, :COLS] = np.cos(angles)
    matrix[1, :COLS, :COLS] = np.sin(angles)
    matrix = matrix.reshape(2 * HALF, HALF)
    high = matrix.astype(jnp.bfloat16)
    low = (matrix - high.astype(np.float32)).astype(jnp.bfloat16)
    columns = np.zeros((HALF, ROWS), np.float32)
    for q in range(9):
        turn = q * at * (2.0 * math.pi / NLON)
        columns[:COLS, q] = np.cos(turn)
        columns[:COLS, 16 + q] = -np.sin(turn)
        wave = q + 16 * at
        wave = np.minimum(wave, NLON - wave)
        sine = np.sin((wave.astype(np.float32) * np.float32(math.pi / NLON)).astype(np.float64))
        sine_sq = (sine.astype(np.float32) * sine.astype(np.float32)).astype(np.float64)
        over = np.where(wave == 0, 1e30, 1.0 / np.where(wave == 0, 1.0, sine_sq))
        columns[:COLS, 32 + q] = over * scale_of(q)
    return np.concatenate([high, low], axis=0), columns


def scale_of(q):
    return (1.0 if q in (0, 8) else 2.0) / NLON


SIN = [math.sin(math.pi * t / 8) for t in range(5)]


def times(value, c, s):
    re, im = value
    return (c * re - s * im, c * im + s * re)


def forward16(x):
    e = [x[p] + x[p + 8] for p in range(8)]
    o = [x[p] - x[p + 8] for p in range(8)]
    e2 = [e[p] + e[p + 4] for p in range(4)]
    o2 = [e[p] - e[p + 4] for p in range(4)]
    a, b = e2[0] + e2[2], e2[1] + e2[3]
    pairs = [None] * 8
    pairs[0] = (a + b, a - b)
    pairs[4] = (e2[0] - e2[2], e2[3] - e2[1])
    root = SIN[2]
    u = (o2[0], -o2[2])
    w = times((o2[1], -o2[3]), root, -root)
    pairs[2] = (u[0] + w[0], u[1] + w[1])
    pairs[6] = (u[0] - w[0], w[1] - u[1])
    d = [times((o[p], -o[p + 4]), SIN[4 - p], -SIN[p]) if p else (o[p], -o[p + 4]) for p in range(4)]
    s02 = (d[0][0] + d[2][0], d[0][1] + d[2][1])
    t02 = (d[0][0] - d[2][0], d[0][1] - d[2][1])
    s13 = (d[1][0] + d[3][0], d[1][1] + d[3][1])
    t13 = (d[1][0] - d[3][0], d[1][1] - d[3][1])
    pairs[1] = (s02[0] + s13[0], s02[1] + s13[1])
    pairs[7] = (s02[0] - s13[0], s13[1] - s02[1])
    pairs[5] = (t02[0] + t13[1], t02[1] - t13[0])
    pairs[3] = (t02[0] - t13[1], -(t02[1] + t13[0]))
    return pairs


def inverse16(pairs):
    z0, z8 = pairs[0]
    a, b = z0 + z8, z0 - z8
    e2 = [a + pairs[4][0], b - pairs[4][1], a - pairs[4][0], b + pairs[4][1]]
    u, v = pairs[2], (pairs[6][0], -pairs[6][1])
    d0 = (u[0] + v[0], u[1] + v[1])
    root = SIN[2]
    d1 = times((u[0] - v[0], u[1] - v[1]), root, root)
    o2 = [d0[0], d1[0], -d0[1], -d1[1]]
    e = [e2[p] + o2[p] for p in range(4)] + [e2[p] - o2[p] for p in range(4)]
    a1, a5 = pairs[1], pairs[5]
    a9, a13 = (pairs[7][0], -pairs[7][1]), (pairs[3][0], -pairs[3][1])
    s19 = (a1[0] + a9[0], a1[1] + a9[1])
    t19 = (a1[0] - a9[0], a1[1] - a9[1])
    s5 = (a5[0] + a13[0], a5[1] + a13[1])
    t5 = (a5[0] - a13[0], a5[1] - a13[1])
    d = [
        (s19[0] + s5[0], s19[1] + s5[1]),
        (t19[0] - t5[1], t19[1] + t5[0]),
        (s19[0] - s5[0], s19[1] - s5[1]),
        (t19[0] + t5[1], t19[1] - t5[0]),
    ]
    d = [times(d[p], SIN[4 - p], SIN[p]) if p else d[p] for p in range(4)]
    o = [d[p][0] for p in range(4)] + [-d[p][1] for p in range(4)]
    return [e[p] + o[p] for p in range(8)] + [e[p] - o[p] for p in range(8)]


def row(i):
    return pl.ds(pl.multiple_of(i * LEV, LEV), LEV)


def lanes_of(shape):
    return lax.broadcasted_iota(jnp.int32, shape, len(shape) - 1)


def ends_kernel(*refs):
    for f in range(3):
        refs[6][f] = refs[f][...]
        refs[7][f] = refs[3 + f][...]


def ends(fields):
    first = pl.BlockSpec((LEV, ROWS), lambda i: (0, 0))
    last = pl.BlockSpec((LEV, ROWS), lambda i: (COLS - 1, 0))
    out = pl.BlockSpec((3, LEV, ROWS), lambda i: (0, 0, 0))
    return pl.pallas_call(
        ends_kernel,
        grid=(1,),
        in_specs=[first] * 3 + [last] * 3,
        out_specs=[out] * 2,
        out_shape=[jax.ShapeDtypeStruct((3, LEV, ROWS), jnp.float32)] * 2,
    )(*fields, *fields)


def widen_kernel(place, first, second, west, east, first_out, second_out):
    even = place[4] == 1
    lane = lanes_of((LEV, ROWS))
    for f in range(4):
        back = 2 if f == 3 else 1
        side_west, side_east = west[min(f, 2)], east[min(f, 2)]
        end = (COLS + 1) % ROWS
        north = (pltpu.roll(side_west, back, 1), pltpu.roll(side_east, end + back, 1))
        south = (side_west, pltpu.roll(side_east, end, 1))
        for source, out, is_north in (
            (first, first_out, even),
            (second, second_out, jnp.logical_not(even)),
        ):
            at_west, at_east = (jnp.where(is_north, a, b) for a, b in zip(north, south))
            out[f, 0] = jnp.where(lane == 0, at_west, source[f, 0])
            out[f, 1] = jnp.where(lane == end, at_east, source[f, 1])


def widen(place, first, second, west, east):
    vmem = pl.BlockSpec(memory_space=pltpu.VMEM)
    shape = jax.ShapeDtypeStruct(first.shape, jnp.float32)
    return pl.pallas_call(
        widen_kernel,
        grid_spec=pltpu.PrefetchScalarGridSpec(
            num_scalar_prefetch=1, grid=(1,), in_specs=[vmem] * 4, out_specs=[vmem] * 2
        ),
        out_shape=[shape] * 2,
    )(place, first, second, west, east)


def pack_kernel(place, h, u, v, first, second, low, high):
    step = pl.program_id(0)

    @pl.when(step == 0)
    def _():
        low[...] = jnp.zeros_like(low)
        high[...] = jnp.zeros_like(high)

    spots = [lanes_of((LEV, ROWS)) + ROWS * part for part in range(2)]
    kept_low = [[low[f, part] for part in range(2)] for f in range(3)]
    kept_high = [[high[f, part] for part in range(2)] for f in range(4)]
    for i in range(PACK):
        spot = step * PACK + i + 1
        masks = [[s == spot + k for s in spots] for k in (-1, 0, 1)]
        for f, field in enumerate((h, u, v)):
            turned = pltpu.roll(field[i * LEV : (i + 1) * LEV, :], lax.rem(spot + 1, ROWS), 1)
            for part in range(2):
                kept_high[f][part] = jnp.where(masks[1][part], turned, kept_high[f][part])
                kept_low[f][part] = jnp.where(masks[2][part], turned, kept_low[f][part])
                if f == 2:
                    kept_high[3][part] = jnp.where(masks[0][part], turned, kept_high[3][part])
    for part in range(2):
        for f in range(3):
            low[f, part] = kept_low[f][part]
        for f in range(4):
            high[f, part] = kept_high[f][part]

    @pl.when(step == pl.num_programs(0) - 1)
    def _():
        even = place[4] == 1
        for f in range(4):
            if f < 3:
                south = shift_lanes([low[f, 0], low[f, 1]], -1)
                north = [high[f, 0], high[f, 1]]
            else:
                south = [jnp.zeros((LEV, ROWS), jnp.float32)] * 2
                north = shift_lanes([high[f, 0], high[f, 1]], 1)
            for part in range(2):
                first[f, part] = jnp.where(even, north[part], south[part])
                second[f, part] = jnp.where(even, south[part], north[part])


def shift_lanes(parts, by):
    turned = [pltpu.roll(part, by % ROWS, 1) for part in parts]
    lane = lanes_of(parts[0].shape)
    fresh = lane == (0 if by > 0 else ROWS - 1)
    return [jnp.where(fresh, turned[1 - i], turned[i]) for i in range(2)]


def pack(place, height, u_wind, v_wind):
    field = pl.BlockSpec((PACK * LEV, ROWS), lambda i, s: (i, 0))
    shape = (4, 2, LEV, ROWS)
    edge = pl.BlockSpec(shape, lambda i, s: (0, 0, 0, 0))
    return pl.pallas_call(
        pack_kernel,
        grid_spec=pltpu.PrefetchScalarGridSpec(
            num_scalar_prefetch=1,
            grid=(COLS // PACK,),
            in_specs=[field, field, field],
            out_specs=[edge, edge],
            scratch_shapes=[pltpu.VMEM(shape, jnp.float32)] * 2,
        ),
        out_shape=[jax.ShapeDtypeStruct(shape, jnp.float32)] * 2,
        cost_estimate=pl.CostEstimate(flops=0, bytes_accessed=4_700_000, transcendentals=0),
    )(place, height, u_wind, v_wind)


def rim_terms(place, first, second, table, terms):
    even, at_north, at_south = place[4] == 1, place[1] == 1, place[2] == 1
    lane = lanes_of((LEV, ROWS))

    def rim(f, part):
        above = jnp.where(even, first[f, part], second[f, part])
        below = jnp.where(even, second[f, part], first[f, part])
        if f == 0:
            return above, below
        turned = -second[3 if f == 2 else f, part]
        across = -second[f, part] if f == 1 else jnp.zeros_like(below)
        return jnp.where(at_north, turned, above), jnp.where(at_south, across, below)

    (h_n, h_s), (u_n, u_s), (v_n, v_s) = (
        zip(*(rim(f, part) for part in range(2))) for f in range(3)
    )
    turn_u, cos_south, diverge = (table[0, i : i + 1, 0:1] for i in (1, 4, 6))
    turn_v = table[0, 2:3, ROWS - 1 : ROWS]
    u_nw, v_se = shift_lanes(u_n, 1), shift_lanes(v_s, -1)
    for part in range(2):
        north = (
            DIFFUSION * h_n[part],
            DIFFUSION * u_n[part],
            DIFFUSION * v_n[part] - GRAV_MERID * h_n[part] - turn_v * (u_n[part] + u_nw[part]),
        )
        south = (
            DIFFUSION * h_s[part] + diverge * cos_south * v_s[part],
            DIFFUSION * u_s[part] + turn_u * (v_s[part] + v_se[part]),
            DIFFUSION * v_s[part],
        )
        for f in range(3):
            after = pltpu.roll(south[f], 1, 1)
            for odd in range(2):
                terms[f, odd, part] = jnp.where(lane % 2 == odd, north[f], after)


def stencil_kernel(
    polar, place, h, u, v, h_west, u_west, v_west, h_east, u_east, v_east, west, east, first, second, table,
    *refs,
):
    outs, (terms, whole) = refs[:-2], refs[-2:]
    step = pl.program_id(0)
    lane = lanes_of((LEV, ROWS))
    edges = (lane == 0) | (lane == ROWS - 1)

    @pl.when(step == 0)
    def _():
        rim_terms(place, first, second, table, terms)

    zonal, turn_u, turn_v, cos_face, cos_south, _, diverge = (
        jnp.broadcast_to(table[0, i : i + 1, :], (LEV, ROWS)) for i in range(7)
    )

    def north(block):
        return jnp.where(lane == ROWS - 1, 0.0, pltpu.roll(block, ROWS - 1, 1))

    def south(block):
        return jnp.where(lane == 0, 0.0, pltpu.roll(block, 1, 1))

    def update(k, odd, carry, blocks_east):
        (t_west, v_south, w_here), (west_h, west_u, west_v) = carry
        mid_h, mid_u, mid_v = middle = [field[row(k), :] for field in (h, u, v)]
        east_h, east_u, east_v = blocks_east
        h_north, h_south = north(mid_h), south(mid_h)
        u_north, u_south = north(mid_u), south(mid_u)
        v_north, v_south_east = north(mid_v), south(east_v)
        t_here = mid_u + u_north
        w_east = east_v + v_south_east
        new_u = (
            mid_u
            - zonal * (east_h - mid_h)
            + turn_u * (w_here + w_east)
            + DIFFUSION * (east_u + west_u + (u_north + u_south) - 4.0 * mid_u)
        )
        new_v = (
            mid_v
            - GRAV_MERID * (h_north - mid_h)
            - turn_v * (t_here + t_west)
            + DIFFUSION * (east_v + west_v + (v_north + v_south) - 4.0 * mid_v)
        )
        new_h = (
            mid_h
            - diverge * (mid_u - west_u + cos_face * mid_v - cos_south * v_south)
            + DIFFUSION * (east_h + west_h + (h_north + h_south) - 4.0 * mid_h)
        )
        spot = step * CHUNK + k + 1
        turn = lax.rem(2 * ROWS - 1 - spot, ROWS)
        results = []
        for f, new in enumerate((new_h, new_u, new_v)):
            term = pltpu.roll(terms[f, odd, spot // ROWS], turn, 1)
            results.append(new + jnp.where(edges, term, 0.0))
        return ((t_here, v_south_east, w_east), middle), results

    def several(base, carry, beyond):
        found = []
        for n in range(AHEAD):
            k = base + n
            if n == AHEAD - 1 and beyond is not None:
                blocks = beyond
            else:
                blocks = [field[row(k + 1), :] for field in (h, u, v)]
            if n == (COLS - 1) % AHEAD:
                is_last = step * CHUNK + k == COLS - 1
                blocks = [jnp.where(is_last, east[f], blocks[f]) for f in range(3)]
            carry, results = update(k, (n + 1) % 2, carry, blocks)
            found.append(results)
        for n, results in enumerate(found):
            for f in range(3):
                whole[f, row(base + n), :] = results[f]
        return carry

    before = [
        jnp.where(step == 0, west[f], field[...]) for f, field in enumerate((h_west, u_west, v_west))
    ]
    here_v = v[row(0), :]
    v_south = south(here_v)
    carry = ((before[1] + north(before[1]), v_south, here_v + v_south), before)
    groups = CHUNK // AHEAD
    carry = lax.fori_loop(
        0, groups - 1, lambda c, carry: several(c * AHEAD, carry, None), carry
    )
    several((groups - 1) * AHEAD, carry, [field[...] for field in (h_east, u_east, v_east)])

    if not polar:
        for f, out in enumerate(outs):
            out[...] = whole[f]
        return

    def turned(f):
        return jnp.transpose(whole[f].reshape(CHUNK, LEV, ROWS), (1, 0, 2))

    uv_out, h_first, h_second = outs
    height = turned(0)
    h_first[...] = height[: LEV // 2]
    h_second[...] = height[LEV // 2 :]
    uv_out[:, 0] = turned(1)
    uv_out[:, 1] = turned(2)


def stencil(polar, place, height, u_wind, v_wind, west, east, first, second, tables):
    block = pl.BlockSpec((CHUNK * LEV, ROWS), lambda i, s: (i, 0))
    one_west = pl.BlockSpec((LEV, ROWS), lambda i, s: (jnp.maximum(i * CHUNK - 1, 0), 0))
    one_east = pl.BlockSpec(
        (LEV, ROWS), lambda i, s: (jnp.minimum((i + 1) * CHUNK, COLS - 1), 0)
    )
    side = pl.BlockSpec((3, LEV, ROWS), lambda i, s: (0, 0, 0))
    edge = pl.BlockSpec((4, 2, LEV, ROWS), lambda i, s: (0, 0, 0, 0))
    sent = pl.BlockSpec((LEV // 2, CHUNK, ROWS), lambda i, s: (0, i, 0))
    pair = pl.BlockSpec((LEV, 2, CHUNK, ROWS), lambda i, s: (0, 0, i, 0))
    own = jax.ShapeDtypeStruct((COLS * LEV, ROWS), jnp.float32)
    full = jax.ShapeDtypeStruct((LEV, 2, TALL, ROWS), jnp.float32)
    half = jax.ShapeDtypeStruct((LEV // 2, TALL, ROWS), jnp.float32)
    fields = (height, u_wind, v_wind)
    return pl.pallas_call(
        functools.partial(stencil_kernel, polar),
        grid_spec=pltpu.PrefetchScalarGridSpec(
            num_scalar_prefetch=1,
            grid=(pl.cdiv(COLS, CHUNK),),
            in_specs=[block] * 3
            + [one_west] * 3
            + [one_east] * 3
            + [side] * 2
            + [edge] * 2
            + [pl.BlockSpec((1, 8, ROWS), lambda i, s: (s[0], 0, 0))],
            out_specs=[pair, sent, sent] if polar else [block] * 3,
            scratch_shapes=[
                pltpu.VMEM((3, 2, 2, LEV, ROWS), jnp.float32),
                pltpu.VMEM((3, CHUNK * LEV, ROWS), jnp.float32),
            ],
        ),
        out_shape=[full, half, half] if polar else [own] * 3,
        compiler_params=pltpu.CompilerParams(vmem_limit_bytes=58 * 1024 * 1024),
        cost_estimate=pl.CostEstimate(
            flops=60_000_000, bytes_accessed=9_000_000, transcendentals=0
        ),
    )(place, *fields, *fields, *fields, west, east, first, second, tables)


def unpack_kernel(
    place, own_u, own_v, own_h, uv, h_first, h_second, u_out, v_out, h_out
):
    def turned(block):
        return jnp.transpose(block, (1, 0, 2)).reshape(SOME * LEV, ROWS)

    @pl.when(place[3] == 1)
    def _():
        u_out[...] = turned(uv[:, 0])
        v_out[...] = turned(uv[:, 1])
        h_out[...] = turned(jnp.concatenate([h_first[...], h_second[...]], 0))

    @pl.when(place[3] == 0)
    def _():
        u_out[...] = own_u[...]
        v_out[...] = own_v[...]
        h_out[...] = own_h[...]


def unpack(place, own_u, own_v, own_h, uv, h_first, h_second):
    def pick(polar):
        return lambda i, s: jnp.where(s[3] == polar, i, 0)

    kept, used = pick(0), pick(1)
    half = pl.BlockSpec((LEV // 2, SOME, ROWS), lambda i, s: (0, used(i, s), 0))
    return pl.pallas_call(
        unpack_kernel,
        grid_spec=pltpu.PrefetchScalarGridSpec(
            num_scalar_prefetch=1,
            grid=(pl.cdiv(COLS, SOME),),
            in_specs=[pl.BlockSpec((SOME * LEV, ROWS), lambda i, s: (kept(i, s), 0))] * 3
            + [pl.BlockSpec((LEV, 2, SOME, ROWS), lambda i, s: (0, 0, used(i, s), 0))]
            + [half] * 2,
            out_specs=[pl.BlockSpec((SOME * LEV, ROWS), lambda i, s: (i, 0))] * 3,
        ),
        out_shape=[jax.ShapeDtypeStruct((COLS * LEV, ROWS), jnp.float32)] * 3,
        compiler_params=pltpu.CompilerParams(vmem_limit_bytes=58 * 1024 * 1024),
        cost_estimate=pl.CostEstimate(
            flops=0, bytes_accessed=24 * COLS * LEV * ROWS, transcendentals=0
        ),
    )(place, own_u, own_v, own_h, uv, h_first, h_second)


def filter_kernel(place, x, matrix, columns, table, out, spectra, waves):
    def column(rows, q):
        return columns[rows, q : q + 1]

    def gather(start, blocks):
        rows = pl.ds(pl.multiple_of(start, 16), 16)
        pairs = forward16(blocks)
        parts = [(pairs[0][0], None)] + pairs[1:] + [(pairs[0][1], None)]
        for q, (re, im) in enumerate(parts):
            if q == 0:
                im = jnp.zeros_like(re)
            else:
                c, s = column(rows, q), column(rows, 16 + q)
                re, im = (c * re, s * re) if im is None else times((re, im), c, s)
            for side, value in enumerate((re, im)):
                high, low = split(value)
                spectra[q, 0, rows, side * ROWS : (side + 1) * ROWS] = high
                spectra[q, 1, rows, side * ROWS : (side + 1) * ROWS] = low

    def fill(c, carry):
        start = pl.multiple_of(c * 16, 16)
        gather(start, [x[p, pl.ds(start, 16), :] for p in range(16)])
        return carry

    full = COLS // 16
    lax.fori_loop(0, full, fill, 0, unroll=full)
    empty = jnp.zeros((HALF - COLS, ROWS), jnp.float32)
    tail = pl.ds(16 * full, COLS % 16)
    gather(16 * full, [jnp.concatenate([x[p, tail, :], empty], 0) for p in range(16)])

    def product(high, low):
        found = jnp.dot(matrix[: 2 * HALF], high, preferred_element_type=jnp.float32)
        found += jnp.dot(matrix[2 * HALF :], high, preferred_element_type=jnp.float32)
        found += jnp.dot(matrix[: 2 * HALF], low, preferred_element_type=jnp.float32)
        cos, sin = found[:HALF], found[HALF:]
        return cos[:, :ROWS], cos[:, ROWS:], sin[:, :ROWS], sin[:, ROWS:]

    ratio = table[0, 5:6, :]
    rows = slice(0, HALF)
    for q in range(9):
        cos_re, cos_im, sin_re, sin_im = product(spectra[q, 0], spectra[q, 1])
        damping = jnp.minimum(ratio * column(rows, 32 + q), scale_of(q))
        re, im = damping * (cos_re + sin_im), damping * (cos_im - sin_re)
        cos_re, cos_im, sin_re, sin_im = product(*split(jnp.concatenate([re, im], 1)))
        re = cos_re - sin_im
        if q:
            im = cos_im + sin_re
            c, s = column(rows, q), column(rows, 16 + q)
            if q < 8:
                waves[q, 1] = c * im - s * re
            re = c * re + s * im
        waves[q, 0] = re

    def give(c, carry):
        rows = pl.ds(pl.multiple_of(c * 8, 8), 8)
        pairs = [(waves[0, 0, rows, :], waves[8, 0, rows, :])]
        pairs += [(waves[q, 0, rows, :], waves[q, 1, rows, :]) for q in range(1, 8)]
        for p, value in enumerate(inverse16(pairs)):
            out[p, rows, :] = value
        return carry

    lax.fori_loop(0, TALL // 8, give, 0, unroll=TALL // 8)


def polar_filter(place, x, tables):
    matrix, columns = fourier_tables()
    field = pl.BlockSpec((LEV, None, TALL, ROWS), lambda i, s: (0, i, 0, 0))
    return pl.pallas_call(
        filter_kernel,
        grid_spec=pltpu.PrefetchScalarGridSpec(
            num_scalar_prefetch=1,
            grid=(x.shape[1],),
            in_specs=[
                field,
                pl.BlockSpec(matrix.shape, lambda i, s: (0, 0)),
                pl.BlockSpec(columns.shape, lambda i, s: (0, 0)),
                pl.BlockSpec((1, 8, ROWS), lambda i, s: (s[0], 0, 0)),
            ],
            out_specs=field,
            scratch_shapes=[
                pltpu.VMEM((9, 2, HALF, 2 * ROWS), jnp.bfloat16),
                pltpu.VMEM((9, 2, HALF, ROWS), jnp.float32),
            ],
        ),
        out_shape=jax.ShapeDtypeStruct(x.shape, jnp.float32),
        compiler_params=pltpu.CompilerParams(vmem_limit_bytes=58 * 1024 * 1024),
        cost_estimate=pl.CostEstimate(
            flops=216 * HALF * HALF * ROWS * x.shape[1], bytes_accessed=3_500_000 * x.shape[1], transcendentals=0
        ),
    )(place, x, jnp.asarray(matrix), jnp.asarray(columns), tables)


BESIDE = ((0, 3), (1, 2), (6, 5), (7, 4))
BEYOND = ((0, 4), (1, 5), (6, 2), (7, 3))


def lent(pairs, turn):
    return [
        (lon * N_LAT + polar, (lon ^ turn) * N_LAT + other)
        for lon in range(N_LON)
        for polar, other in pairs
    ]


def returned(pairs, turn):
    return [(j, i) for i, j in lent(pairs, turn)]


def partner(band, pairs):
    return sum(jnp.where(band == other, polar, 0) for polar, other in pairs).astype(jnp.int32)


def unused(like):
    return pl.pallas_call(
        lambda out: None,
        out_specs=pl.BlockSpec(memory_space=pl.ANY),
        out_shape=jax.ShapeDtypeStruct(like.shape, like.dtype),
    )()


def shards(u_wind, v_wind, height):
    band = lax.axis_index("lat")
    is_polar = (band < N_LAT // 4) | (band >= N_LAT - N_LAT // 4)
    even = band % 2 == 0
    place = jnp.stack([band, band == N_LAT - 1, band == 0, is_polar, even]).astype(jnp.int32)
    tables = jnp.asarray(latitude_tables())
    fields = [jnp.swapaxes(x, 0, 1) for x in (height, u_wind, v_wind)]
    flat = [x.reshape(COLS * LEV, ROWS) for x in fields]
    east_to = [(i, (i + 1) % N_LON) for i in range(N_LON)]
    initial, last = ends(flat)
    west = lax.ppermute(last, "lon", east_to)
    east = lax.ppermute(initial, "lon", [(j, i) for i, j in east_to])
    first, second = pack(place, *flat)
    first, second = widen(place, first, second, west, east)
    swap = [(i, i ^ 1) for i in range(N_LAT)]
    first = lax.ppermute(first, "lat", swap)
    routes = [(lon, i, lon, i + 1) for lon in range(N_LON) for i in range(1, N_LAT - 1, 2)]
    routes += [(lon, i + 1, lon, i) for lon, i, _, _ in routes]
    routes += [
        (lon, i, (lon + N_LON // 2) % N_LON, i) for lon in range(N_LON) for i in (0, N_LAT - 1)
    ]
    second = lax.ppermute(
        second,
        AXES,
        [(a * N_LAT + b, c * N_LAT + d) for a, b, c, d in routes],
    )
    def exchange(value):
        return lax.all_to_all(value, "lon", split_axis=0, concat_axis=0, tiled=True)

    def keep(circles, h_first, h_second):
        return polar_filter(place, circles, tables), unused(h_first), unused(h_second)

    def help_out(circles, h_first, h_second):
        circles = exchange(jnp.concatenate([h_first, h_second], 0))
        lender = jnp.where(
            lax.axis_index("lon") < N_LON // 2, partner(band, BESIDE), partner(band, BEYOND)
        )
        h = exchange(polar_filter(lender.reshape(1), circles[:, None], tables)[:, 0])
        return unused(uv), h[: LEV // 2], h[LEV // 2 :]

    inputs = (place, *flat, west, east, first, second, tables)
    whole = jax.ShapeDtypeStruct((LEV, 2, TALL, ROWS), jnp.float32)
    half = jax.ShapeDtypeStruct((LEV // 2, TALL, ROWS), jnp.float32)
    own = jax.ShapeDtypeStruct((COLS * LEV, ROWS), jnp.float32)
    uv, h_first, h_second = lax.cond(
        is_polar,
        lambda *inputs: tuple(stencil(True, *inputs)),
        lambda *inputs: (unused(whole), unused(half), unused(half)),
        *inputs,
    )

    h_first = lax.ppermute(h_first, AXES, lent(BESIDE, 0))
    h_second = lax.ppermute(h_second, AXES, lent(BEYOND, N_LON // 2))
    circles, own_h, own_u, own_v = lax.cond(
        is_polar,
        lambda uv, *inputs: (exchange(uv), unused(own), unused(own), unused(own)),
        lambda uv, *inputs: (unused(uv), *stencil(False, *inputs)),
        uv, *inputs,
    )
    circles, h_first, h_second = lax.cond(is_polar, keep, help_out, circles, h_first, h_second)
    h_first = lax.ppermute(h_first, AXES, returned(BESIDE, 0))
    h_second = lax.ppermute(h_second, AXES, returned(BEYOND, N_LON // 2))
    uv = lax.cond(is_polar, exchange, unused, circles)
    result = unpack(place, own_u, own_v, own_h, uv, h_first, h_second)
    return tuple(jnp.swapaxes(x.reshape(COLS, LEV, ROWS), 0, 1) for x in result)


def solution(mesh):
    placed = (P(None, "lon", "lat"),) * 3
    return jax.shard_map(shards, mesh=mesh, in_specs=placed, out_specs=placed, check_vma=False)
```

```python
import functools
import math

import jax
import jax.numpy as jnp
import numpy as np
from jax import lax
from jax.experimental import pallas as pl
from jax.experimental.pallas import tpu as pltpu
from jax.sharding import PartitionSpec as P

N_LON = 16
N_LAT = 8
LEV = 16
COLS = 180
ROWS = 128
NLON = N_LON * COLS
NLAT = N_LAT * ROWS
HALF = 192
TALL = 184
PACK = 90
CHUNK = 64
SOME = 96
AHEAD = 32
AXES = ("lon", "lat")

GRAV_ZONAL = 0.3
GRAV_MERID = 0.6
CORIOLIS = 0.8
DIVERGENCE = 0.3
DIFFUSION = 0.08


def latitude_tables():
    f32 = np.float32
    index = np.arange(NLAT).astype(f32)
    step = f32(math.pi / NLAT)

    def sine(angle):
        return np.sin(angle.astype(np.float64)).astype(f32)

    def cosine(angle):
        return np.cos(angle.astype(np.float64)).astype(f32)

    center = (index + f32(0.5)) * step
    face = (index + f32(1.0)) * step
    cos_center = sine(center)
    sin_center = -cosine(center)
    sin_face = -cosine(face)
    cos_face = np.where(index + 1 < NLAT, sine(face), f32(0.0))
    cos_south = sine(index * step)
    ratio = f32(2.0) * cos_center * cos_center
    table = np.stack(
        [
            GRAV_ZONAL / cos_center.astype(np.float64),
            CORIOLIS * 0.25 * sin_center.astype(np.float64),
            CORIOLIS * 0.25 * sin_face.astype(np.float64),
            cos_face,
            cos_south,
            ratio,
            DIVERGENCE / cos_center.astype(np.float64),
            np.zeros(NLAT),
        ]
    ).astype(f32)
    return np.ascontiguousarray(table.reshape(8, N_LAT, ROWS).transpose(1, 0, 2))


def split(value):
    high = value.astype(jnp.bfloat16)
    return high, (value - high.astype(value.dtype)).astype(jnp.bfloat16)


@functools.cache
def fourier_tables():
    at = np.arange(COLS)
    angles = (at[:, None] * at[None, :] % COLS) * (2.0 * math.pi / COLS)
    matrix = np.zeros((2, HALF, HALF), np.float32)
    matrix[0, :COLS, :COLS] = np.cos(angles)
    matrix[1, :COLS, :COLS] = np.sin(angles)
    matrix = matrix.reshape(2 * HALF, HALF)
    high = matrix.astype(jnp.bfloat16)
    low = (matrix - high.astype(np.float32)).astype(jnp.bfloat16)
    columns = np.zeros((HALF, ROWS), np.float32)
    for q in range(9):
        turn = q * at * (2.0 * math.pi / NLON)
        columns[:COLS, q] = np.cos(turn)
        columns[:COLS, 16 + q] = -np.sin(turn)
        wave = q + 16 * at
        wave = np.minimum(wave, NLON - wave)
        sine = np.sin((wave.astype(np.float32) * np.float32(math.pi / NLON)).astype(np.float64))
        sine_sq = (sine.astype(np.float32) * sine.astype(np.float32)).astype(np.float64)
        over = np.where(wave == 0, 1e30, 1.0 / np.where(wave == 0, 1.0, sine_sq))
        columns[:COLS, 32 + q] = over * scale_of(q)
    return np.concatenate([high, low], axis=0), columns


def scale_of(q):
    return (1.0 if q in (0, 8) else 2.0) / NLON


SIN = [math.sin(math.pi * t / 8) for t in range(5)]


def times(value, c, s):
    re, im = value
    return (c * re - s * im, c * im + s * re)


def forward16(x):
    e = [x[p] + x[p + 8] for p in range(8)]
    o = [x[p] - x[p + 8] for p in range(8)]
    e2 = [e[p] + e[p + 4] for p in range(4)]
    o2 = [e[p] - e[p + 4] for p in range(4)]
    a, b = e2[0] + e2[2], e2[1] + e2[3]
    pairs = [None] * 8
    pairs[0] = (a + b, a - b)
    pairs[4] = (e2[0] - e2[2], e2[3] - e2[1])
    root = SIN[2]
    u = (o2[0], -o2[2])
    w = times((o2[1], -o2[3]), root, -root)
    pairs[2] = (u[0] + w[0], u[1] + w[1])
    pairs[6] = (u[0] - w[0], w[1] - u[1])
    d = [times((o[p], -o[p + 4]), SIN[4 - p], -SIN[p]) if p else (o[p], -o[p + 4]) for p in range(4)]
    s02 = (d[0][0] + d[2][0], d[0][1] + d[2][1])
    t02 = (d[0][0] - d[2][0], d[0][1] - d[2][1])
    s13 = (d[1][0] + d[3][0], d[1][1] + d[3][1])
    t13 = (d[1][0] - d[3][0], d[1][1] - d[3][1])
    pairs[1] = (s02[0] + s13[0], s02[1] + s13[1])
    pairs[7] = (s02[0] - s13[0], s13[1] - s02[1])
    pairs[5] = (t02[0] + t13[1], t02[1] - t13[0])
    pairs[3] = (t02[0] - t13[1], -(t02[1] + t13[0]))
    return pairs


def inverse16(pairs):
    z0, z8 = pairs[0]
    a, b = z0 + z8, z0 - z8
    e2 = [a + pairs[4][0], b - pairs[4][1], a - pairs[4][0], b + pairs[4][1]]
    u, v = pairs[2], (pairs[6][0], -pairs[6][1])
    d0 = (u[0] + v[0], u[1] + v[1])
    root = SIN[2]
    d1 = times((u[0] - v[0], u[1] - v[1]), root, root)
    o2 = [d0[0], d1[0], -d0[1], -d1[1]]
    e = [e2[p] + o2[p] for p in range(4)] + [e2[p] - o2[p] for p in range(4)]
    a1, a5 = pairs[1], pairs[5]
    a9, a13 = (pairs[7][0], -pairs[7][1]), (pairs[3][0], -pairs[3][1])
    s19 = (a1[0] + a9[0], a1[1] + a9[1])
    t19 = (a1[0] - a9[0], a1[1] - a9[1])
    s5 = (a5[0] + a13[0], a5[1] + a13[1])
    t5 = (a5[0] - a13[0], a5[1] - a13[1])
    d = [
        (s19[0] + s5[0], s19[1] + s5[1]),
        (t19[0] - t5[1], t19[1] + t5[0]),
        (s19[0] - s5[0], s19[1] - s5[1]),
        (t19[0] + t5[1], t19[1] - t5[0]),
    ]
    d = [times(d[p], SIN[4 - p], SIN[p]) if p else d[p] for p in range(4)]
    o = [d[p][0] for p in range(4)] + [-d[p][1] for p in range(4)]
    return [e[p] + o[p] for p in range(8)] + [e[p] - o[p] for p in range(8)]


def row(i):
    return pl.ds(pl.multiple_of(i * LEV, LEV), LEV)


def lanes_of(shape):
    return lax.broadcasted_iota(jnp.int32, shape, len(shape) - 1)


def pack_kernel(place, h, u, v, first, second, low, high):
    step = pl.program_id(0)

    @pl.when(step == 0)
    def _():
        low[...] = jnp.zeros_like(low)
        high[...] = jnp.zeros_like(high)

    spots = [lanes_of((LEV, ROWS)) + ROWS * part for part in range(2)]
    kept_low = [[low[f, part] for part in range(2)] for f in range(3)]
    kept_high = [[high[f, part] for part in range(2)] for f in range(4)]
    for i in range(PACK):
        spot = step * PACK + i + 1
        masks = [[s == spot + k for s in spots] for k in (-1, 0, 1)]
        for f, field in enumerate((h, u, v)):
            turned = pltpu.roll(field[i * LEV : (i + 1) * LEV, :], lax.rem(spot + 1, ROWS), 1)
            for part in range(2):
                kept_high[f][part] = jnp.where(masks[1][part], turned, kept_high[f][part])
                kept_low[f][part] = jnp.where(masks[2][part], turned, kept_low[f][part])
                if f == 2:
                    kept_high[3][part] = jnp.where(masks[0][part], turned, kept_high[3][part])
    for part in range(2):
        for f in range(3):
            low[f, part] = kept_low[f][part]
        for f in range(4):
            high[f, part] = kept_high[f][part]

    @pl.when(step == pl.num_programs(0) - 1)
    def _():
        even = place[4] == 1
        for f in range(4):
            if f < 3:
                south = shift_lanes([low[f, 0], low[f, 1]], -1)
                north = [high[f, 0], high[f, 1]]
            else:
                south = [jnp.zeros((LEV, ROWS), jnp.float32)] * 2
                north = shift_lanes([high[f, 0], high[f, 1]], 1)
            for part in range(2):
                first[f, part] = jnp.where(even, north[part], south[part])
                second[f, part] = jnp.where(even, south[part], north[part])


def shift_lanes(parts, by):
    turned = [pltpu.roll(part, by % ROWS, 1) for part in parts]
    lane = lanes_of(parts[0].shape)
    fresh = lane == (0 if by > 0 else ROWS - 1)
    return [jnp.where(fresh, turned[1 - i], turned[i]) for i in range(2)]


def pack(place, height, u_wind, v_wind):
    field = pl.BlockSpec((PACK * LEV, ROWS), lambda i, s: (i, 0))
    shape = (4, 2, LEV, ROWS)
    edge = pl.BlockSpec(shape, lambda i, s: (0, 0, 0, 0))
    return pl.pallas_call(
        pack_kernel,
        grid_spec=pltpu.PrefetchScalarGridSpec(
            num_scalar_prefetch=1,
            grid=(COLS // PACK,),
            in_specs=[field, field, field],
            out_specs=[edge, edge],
            scratch_shapes=[pltpu.VMEM(shape, jnp.float32)] * 2,
        ),
        out_shape=[jax.ShapeDtypeStruct(shape, jnp.float32)] * 2,
        cost_estimate=pl.CostEstimate(flops=0, bytes_accessed=4_700_000, transcendentals=0),
    )(place, height, u_wind, v_wind)


def rim_terms(place, first, second, table, terms, beside):
    even, at_north, at_south = place[4] == 1, place[1] == 1, place[2] == 1
    lane = lanes_of((LEV, ROWS))

    def rim(f, part):
        above = jnp.where(even, first[f, part], second[f, part])
        below = jnp.where(even, second[f, part], first[f, part])
        if f == 0:
            return above, below
        turned = -second[3 if f == 2 else f, part]
        across = -second[f, part] if f == 1 else jnp.zeros_like(below)
        return jnp.where(at_north, turned, above), jnp.where(at_south, across, below)

    (h_n, h_s), (u_n, u_s), (v_n, v_s) = (
        zip(*(rim(f, part) for part in range(2))) for f in range(3)
    )
    turn_u, cos_south, diverge = (table[0, i : i + 1, 0:1] for i in (1, 4, 6))
    turn_v = table[0, 2:3, ROWS - 1 : ROWS]
    u_nw, v_se = shift_lanes(u_n, 1), shift_lanes(v_s, -1)
    for part in range(2):
        north = (
            DIFFUSION * h_n[part],
            DIFFUSION * u_n[part],
            DIFFUSION * v_n[part] - GRAV_MERID * h_n[part] - turn_v * (u_n[part] + u_nw[part]),
        )
        south = (
            DIFFUSION * h_s[part] + diverge * cos_south * v_s[part],
            DIFFUSION * u_s[part] + turn_u * (v_s[part] + v_se[part]),
            DIFFUSION * v_s[part],
        )
        for f in range(3):
            after = pltpu.roll(south[f], 1, 1)
            for odd in range(2):
                terms[f, odd, part] = jnp.where(lane % 2 == odd, north[f], after)
    last = pltpu.roll(u_n[1], (ROWS - 1 - COLS) % ROWS, 1)
    beside[0] = jnp.where(lane == ROWS - 1, -turn_v * last, 0.0)
    beside[1] = jnp.where(lane == 0, turn_u * pltpu.roll(v_s[0], ROWS - 1, 1), 0.0)


def stencil_kernel(
    polar, place, h, u, v, h_west, u_west, v_west, h_east, u_east, v_east, first, second, table,
    *refs,
):
    outs, (terms, whole, beside, sides) = refs[:-4], refs[-4:]
    step = pl.program_id(0)
    lane = lanes_of((LEV, ROWS))
    edges = (lane == 0) | (lane == ROWS - 1)

    @pl.when(step == 0)
    def _():
        rim_terms(place, first, second, table, terms, beside)

    zonal, turn_u, turn_v, cos_face, cos_south, _, diverge = (
        jnp.broadcast_to(table[0, i : i + 1, :], (LEV, ROWS)) for i in range(7)
    )

    def north(block):
        return jnp.where(lane == ROWS - 1, 0.0, pltpu.roll(block, ROWS - 1, 1))

    def south(block):
        return jnp.where(lane == 0, 0.0, pltpu.roll(block, 1, 1))

    def update(k, odd, carry, blocks_east):
        (t_west, v_south, w_here), (west_h, west_u, west_v) = carry
        mid_h, mid_u, mid_v = middle = [field[row(k), :] for field in (h, u, v)]
        east_h, east_u, east_v = blocks_east
        h_north, h_south = north(mid_h), south(mid_h)
        u_north, u_south = north(mid_u), south(mid_u)
        v_north, v_south_east = north(mid_v), south(east_v)
        t_here = mid_u + u_north
        w_east = east_v + v_south_east
        new_u = (
            mid_u
            - zonal * (east_h - mid_h)
            + turn_u * (w_here + w_east)
            + DIFFUSION * (east_u + west_u + (u_north + u_south) - 4.0 * mid_u)
        )
        new_v = (
            mid_v
            - GRAV_MERID * (h_north - mid_h)
            - turn_v * (t_here + t_west)
            + DIFFUSION * (east_v + west_v + (v_north + v_south) - 4.0 * mid_v)
        )
        new_h = (
            mid_h
            - diverge * (mid_u - west_u + cos_face * mid_v - cos_south * v_south)
            + DIFFUSION * (east_h + west_h + (h_north + h_south) - 4.0 * mid_h)
        )
        spot = step * CHUNK + k + 1
        turn = lax.rem(2 * ROWS - 1 - spot, ROWS)
        results = []
        for f, new in enumerate((new_h, new_u, new_v)):
            term = pltpu.roll(terms[f, odd, spot // ROWS], turn, 1)
            results.append(new + jnp.where(edges, term, 0.0))
        return ((t_here, v_south_east, w_east), middle), results

    def several(base, carry, beyond):
        found = []
        for n in range(AHEAD):
            k = base + n
            if n == AHEAD - 1 and beyond is not None:
                blocks = beyond
            else:
                blocks = [field[row(k + 1), :] for field in (h, u, v)]
            if n == (COLS - 1) % AHEAD:
                is_last = step * CHUNK + k == COLS - 1
                blocks = [jnp.where(is_last, 0.0, block) for block in blocks]
            carry, results = update(k, (n + 1) % 2, carry, blocks)
            found.append(results)
        for n, results in enumerate(found):
            for f in range(3):
                whole[f, row(base + n), :] = results[f]
        return carry

    before = [
        jnp.where(step == 0, 0.0, field[...]) for field in (h_west, u_west, v_west)
    ]
    here_v = v[row(0), :]
    v_south = south(here_v)
    carry = ((before[1] + north(before[1]), v_south, here_v + v_south), before)
    groups = CHUNK // AHEAD
    carry = lax.fori_loop(
        0, groups - 1, lambda c, carry: several(c * AHEAD, carry, None), carry
    )
    several((groups - 1) * AHEAD, carry, [field[...] for field in (h_east, u_east, v_east)])

    @pl.when(step == 0)
    def _():
        mid_h, mid_u, mid_v = (field[row(0), :] for field in (h, u, v))
        sides[1, 0] = DIFFUSION * mid_h
        sides[1, 1] = turn_u * (mid_v + south(mid_v)) + beside[1] - zonal * mid_h + DIFFUSION * mid_u
        sides[1, 2] = DIFFUSION * mid_v

    @pl.when(step == pl.num_programs(0) - 1)
    def _():
        end = (COLS - 1) % CHUNK
        mid_h, mid_u, mid_v = (field[row(end), :] for field in (h, u, v))
        sides[0, 0] = diverge * mid_u + DIFFUSION * mid_h
        sides[0, 1] = DIFFUSION * mid_u
        sides[0, 2] = DIFFUSION * mid_v - turn_v * (mid_u + north(mid_u)) + beside[0]
        if polar:
            for f in range(3):
                for side in range(2):
                    whole[f, row(end + 1 + side), :] = sides[side, f]

    if not polar:
        for f in range(3):
            outs[f][...] = whole[f]
        for side in range(2):
            outs[3 + side][...] = sides[side]
        return

    def turned(f):
        return jnp.transpose(whole[f].reshape(CHUNK, LEV, ROWS), (1, 0, 2))

    uv_out, h_first, h_second = outs
    height = turned(0)
    h_first[...] = height[: LEV // 2]
    h_second[...] = height[LEV // 2 :]
    uv_out[:, 0] = turned(1)
    uv_out[:, 1] = turned(2)


def stencil(polar, place, height, u_wind, v_wind, first, second, tables):
    block = pl.BlockSpec((CHUNK * LEV, ROWS), lambda i, s: (i, 0))
    one_west = pl.BlockSpec((LEV, ROWS), lambda i, s: (jnp.maximum(i * CHUNK - 1, 0), 0))
    one_east = pl.BlockSpec(
        (LEV, ROWS), lambda i, s: (jnp.minimum((i + 1) * CHUNK, COLS - 1), 0)
    )
    side = pl.BlockSpec((3, LEV, ROWS), lambda i, s: (0, 0, 0))
    edge = pl.BlockSpec((4, 2, LEV, ROWS), lambda i, s: (0, 0, 0, 0))
    sent = pl.BlockSpec((LEV // 2, CHUNK, ROWS), lambda i, s: (0, i, 0))
    pair = pl.BlockSpec((LEV, 2, CHUNK, ROWS), lambda i, s: (0, 0, i, 0))
    own = jax.ShapeDtypeStruct((COLS * LEV, ROWS), jnp.float32)
    full = jax.ShapeDtypeStruct((LEV, 2, TALL, ROWS), jnp.float32)
    half = jax.ShapeDtypeStruct((LEV // 2, TALL, ROWS), jnp.float32)
    ends = jax.ShapeDtypeStruct((3, LEV, ROWS), jnp.float32)
    fields = (height, u_wind, v_wind)
    return pl.pallas_call(
        functools.partial(stencil_kernel, polar),
        grid_spec=pltpu.PrefetchScalarGridSpec(
            num_scalar_prefetch=1,
            grid=(pl.cdiv(COLS, CHUNK),),
            in_specs=[block] * 3
            + [one_west] * 3
            + [one_east] * 3
            + [edge] * 2
            + [pl.BlockSpec((1, 8, ROWS), lambda i, s: (s[0], 0, 0))],
            out_specs=[pair, sent, sent] if polar else [block] * 3 + [side] * 2,
            scratch_shapes=[
                pltpu.VMEM((3, 2, 2, LEV, ROWS), jnp.float32),
                pltpu.VMEM((3, CHUNK * LEV, ROWS), jnp.float32),
                pltpu.VMEM((2, LEV, ROWS), jnp.float32),
                pltpu.VMEM((2, 3, LEV, ROWS), jnp.float32),
            ],
        ),
        out_shape=[full, half, half] if polar else [own] * 3 + [ends] * 2,
        compiler_params=pltpu.CompilerParams(vmem_limit_bytes=58 * 1024 * 1024),
        cost_estimate=pl.CostEstimate(
            flops=60_000_000, bytes_accessed=9_000_000, transcendentals=0
        ),
    )(place, *fields, *fields, *fields, first, second, tables)


def unpack_kernel(
    place, own_u, own_v, own_h, west, east, uv, h_first, h_second, u_out, v_out, h_out
):
    def turned(block):
        return jnp.transpose(block, (1, 0, 2)).reshape(SOME * LEV, ROWS)

    @pl.when(place[3] == 1)
    def _():
        u_out[...] = turned(uv[:, 0])
        v_out[...] = turned(uv[:, 1])
        h_out[...] = turned(jnp.concatenate([h_first[...], h_second[...]], 0))

    @pl.when(place[3] == 0)
    def _():
        u_out[...] = own_u[...]
        v_out[...] = own_v[...]
        h_out[...] = own_h[...]
        end = row((COLS - 1) % SOME)
        for f, out in enumerate((h_out, u_out, v_out)):

            @pl.when(pl.program_id(0) == 0)
            def _(f=f, out=out):
                out[row(0), :] += west[f]

            @pl.when(pl.program_id(0) == (COLS - 1) // SOME)
            def _(f=f, out=out):
                out[end, :] += east[f]


def unpack(place, own_u, own_v, own_h, west, east, uv, h_first, h_second):
    def pick(polar):
        return lambda i, s: jnp.where(s[3] == polar, i, 0)

    kept, used = pick(0), pick(1)
    half = pl.BlockSpec((LEV // 2, SOME, ROWS), lambda i, s: (0, used(i, s), 0))
    return pl.pallas_call(
        unpack_kernel,
        grid_spec=pltpu.PrefetchScalarGridSpec(
            num_scalar_prefetch=1,
            grid=(pl.cdiv(COLS, SOME),),
            in_specs=[pl.BlockSpec((SOME * LEV, ROWS), lambda i, s: (kept(i, s), 0))] * 3
            + [pl.BlockSpec((3, LEV, ROWS), lambda i, s: (0, 0, 0))] * 2
            + [pl.BlockSpec((LEV, 2, SOME, ROWS), lambda i, s: (0, 0, used(i, s), 0))]
            + [half] * 2,
            out_specs=[pl.BlockSpec((SOME * LEV, ROWS), lambda i, s: (i, 0))] * 3,
        ),
        out_shape=[jax.ShapeDtypeStruct((COLS * LEV, ROWS), jnp.float32)] * 3,
        compiler_params=pltpu.CompilerParams(vmem_limit_bytes=58 * 1024 * 1024),
        cost_estimate=pl.CostEstimate(
            flops=0, bytes_accessed=24 * COLS * LEV * ROWS, transcendentals=0
        ),
    )(place, own_u, own_v, own_h, west, east, uv, h_first, h_second)


def filter_kernel(place, x, matrix, columns, table, out, spectra, waves):
    def column(rows, q):
        return columns[rows, q : q + 1]

    def gather(start, blocks):
        rows = pl.ds(pl.multiple_of(start, 16), 16)
        pairs = forward16(blocks)
        parts = [(pairs[0][0], None)] + pairs[1:] + [(pairs[0][1], None)]
        for q, (re, im) in enumerate(parts):
            if q == 0:
                im = jnp.zeros_like(re)
            else:
                c, s = column(rows, q), column(rows, 16 + q)
                re, im = (c * re, s * re) if im is None else times((re, im), c, s)
            for side, value in enumerate((re, im)):
                high, low = split(value)
                spectra[q, 0, rows, side * ROWS : (side + 1) * ROWS] = high
                spectra[q, 1, rows, side * ROWS : (side + 1) * ROWS] = low

    at = lax.broadcasted_iota(jnp.int32, (16, ROWS), 0)

    def with_beside(blocks, spot, source, distance):
        return [
            block + jnp.where(at == spot, x[(p + distance) % 16, source : source + 1, :], 0.0)
            for p, block in enumerate(blocks)
        ]

    gather(0, with_beside([x[p, 0:16, :] for p in range(16)], 0, COLS, -1))

    def fill(c, carry):
        start = pl.multiple_of(c * 16, 16)
        gather(start, [x[p, pl.ds(start, 16), :] for p in range(16)])
        return carry

    full = COLS // 16
    lax.fori_loop(1, full, fill, 0, unroll=full - 1)
    empty = jnp.zeros((HALF - COLS, ROWS), jnp.float32)
    tail = pl.ds(16 * full, COLS % 16)
    blocks = [jnp.concatenate([x[p, tail, :], empty], 0) for p in range(16)]
    gather(16 * full, with_beside(blocks, COLS % 16 - 1, COLS + 1, 1))

    def product(high, low):
        found = jnp.dot(matrix[: 2 * HALF], high, preferred_element_type=jnp.float32)
        found += jnp.dot(matrix[2 * HALF :], high, preferred_element_type=jnp.float32)
        found += jnp.dot(matrix[: 2 * HALF], low, preferred_element_type=jnp.float32)
        cos, sin = found[:HALF], found[HALF:]
        return cos[:, :ROWS], cos[:, ROWS:], sin[:, :ROWS], sin[:, ROWS:]

    ratio = table[0, 5:6, :]
    rows = slice(0, HALF)
    for q in range(9):
        cos_re, cos_im, sin_re, sin_im = product(spectra[q, 0], spectra[q, 1])
        damping = jnp.minimum(ratio * column(rows, 32 + q), scale_of(q))
        re, im = damping * (cos_re + sin_im), damping * (cos_im - sin_re)
        cos_re, cos_im, sin_re, sin_im = product(*split(jnp.concatenate([re, im], 1)))
        re = cos_re - sin_im
        if q:
            im = cos_im + sin_re
            c, s = column(rows, q), column(rows, 16 + q)
            if q < 8:
                waves[q, 1] = c * im - s * re
            re = c * re + s * im
        waves[q, 0] = re

    def give(c, carry):
        rows = pl.ds(pl.multiple_of(c * 8, 8), 8)
        pairs = [(waves[0, 0, rows, :], waves[8, 0, rows, :])]
        pairs += [(waves[q, 0, rows, :], waves[q, 1, rows, :]) for q in range(1, 8)]
        for p, value in enumerate(inverse16(pairs)):
            out[p, rows, :] = value
        return carry

    lax.fori_loop(0, TALL // 8, give, 0, unroll=TALL // 8)


def polar_filter(place, x, tables):
    matrix, columns = fourier_tables()
    field = pl.BlockSpec((LEV, None, TALL, ROWS), lambda i, s: (0, i, 0, 0))
    return pl.pallas_call(
        filter_kernel,
        grid_spec=pltpu.PrefetchScalarGridSpec(
            num_scalar_prefetch=1,
            grid=(x.shape[1],),
            in_specs=[
                field,
                pl.BlockSpec(matrix.shape, lambda i, s: (0, 0)),
                pl.BlockSpec(columns.shape, lambda i, s: (0, 0)),
                pl.BlockSpec((1, 8, ROWS), lambda i, s: (s[0], 0, 0)),
            ],
            out_specs=field,
            scratch_shapes=[
                pltpu.VMEM((9, 2, HALF, 2 * ROWS), jnp.bfloat16),
                pltpu.VMEM((9, 2, HALF, ROWS), jnp.float32),
            ],
        ),
        out_shape=jax.ShapeDtypeStruct(x.shape, jnp.float32),
        compiler_params=pltpu.CompilerParams(vmem_limit_bytes=28 * 1024 * 1024),
        cost_estimate=pl.CostEstimate(
            flops=216 * HALF * HALF * ROWS * x.shape[1], bytes_accessed=3_500_000 * x.shape[1], transcendentals=0
        ),
    )(place, x, jnp.asarray(matrix), jnp.asarray(columns), tables)


BESIDE = ((0, 3), (1, 2), (6, 5), (7, 4))
BEYOND = ((0, 4), (1, 5), (6, 2), (7, 3))


def lent(pairs, turn):
    return [
        (lon * N_LAT + polar, (lon ^ turn) * N_LAT + other)
        for lon in range(N_LON)
        for polar, other in pairs
    ]


def returned(pairs, turn):
    return [(j, i) for i, j in lent(pairs, turn)]


def partner(band, pairs):
    return sum(jnp.where(band == other, polar, 0) for polar, other in pairs).astype(jnp.int32)


def unused(like):
    return pl.pallas_call(
        lambda out: None,
        out_specs=pl.BlockSpec(memory_space=pl.ANY),
        out_shape=jax.ShapeDtypeStruct(like.shape, like.dtype),
    )()


def shards(u_wind, v_wind, height):
    band = lax.axis_index("lat")
    is_polar = (band < N_LAT // 4) | (band >= N_LAT - N_LAT // 4)
    even = band % 2 == 0
    place = jnp.stack([band, band == N_LAT - 1, band == 0, is_polar, even]).astype(jnp.int32)
    tables = jnp.asarray(latitude_tables())
    fields = [jnp.swapaxes(x, 0, 1) for x in (height, u_wind, v_wind)]
    flat = [x.reshape(COLS * LEV, ROWS) for x in fields]
    first, second = pack(place, *flat)
    swap = [(i, i ^ 1) for i in range(N_LAT)]
    first = lax.ppermute(first, "lat", swap)
    routes = [(lon, i, lon, i + 1) for lon in range(N_LON) for i in range(1, N_LAT - 1, 2)]
    routes += [(lon, i + 1, lon, i) for lon, i, _, _ in routes]
    routes += [
        (lon, i, (lon + N_LON // 2) % N_LON, i) for lon in range(N_LON) for i in (0, N_LAT - 1)
    ]
    second = lax.ppermute(
        second,
        AXES,
        [(a * N_LAT + b, c * N_LAT + d) for a, b, c, d in routes],
    )
    def exchange(value):
        return lax.all_to_all(value, "lon", split_axis=0, concat_axis=0, tiled=True)

    def help_out(h_first, h_second):
        circles = exchange(jnp.concatenate([h_first, h_second], 0))
        lender = jnp.where(
            lax.axis_index("lon") < N_LON // 2, partner(band, BESIDE), partner(band, BEYOND)
        )
        smooth = polar_filter(lender.reshape(1), circles[:, None], tables)[:, 0]
        h = exchange(smooth)
        return h[: LEV // 2], h[LEV // 2 :]

    inputs = (place, *flat, first, second, tables)
    whole = jax.ShapeDtypeStruct((LEV, 2, TALL, ROWS), jnp.float32)
    half = jax.ShapeDtypeStruct((LEV // 2, TALL, ROWS), jnp.float32)
    own = jax.ShapeDtypeStruct((COLS * LEV, ROWS), jnp.float32)
    ends = jax.ShapeDtypeStruct((3, LEV, ROWS), jnp.float32)
    uv, h_first, h_second = lax.cond(
        is_polar,
        lambda *inputs: tuple(stencil(True, *inputs)),
        lambda *inputs: (unused(whole), unused(half), unused(half)),
        *inputs,
    )

    h_first = lax.ppermute(h_first, AXES, lent(BESIDE, 0))
    h_second = lax.ppermute(h_second, AXES, lent(BEYOND, N_LON // 2))
    circles, own_h, own_u, own_v, west, east = lax.cond(
        is_polar,
        lambda uv, *inputs: (
            polar_filter(place, exchange(uv), tables),
            *(unused(like) for like in (own, own, own, ends, ends)),
        ),
        lambda uv, *inputs: (unused(uv), *stencil(False, *inputs)),
        uv, *inputs,
    )
    h_first, h_second, circles = lax.optimization_barrier((h_first, h_second, circles))
    h_first, h_second = lax.cond(
        is_polar, lambda *parts: tuple(unused(part) for part in parts), help_out, h_first, h_second
    )
    h_first = lax.ppermute(h_first, AXES, returned(BESIDE, 0))
    h_second = lax.ppermute(h_second, AXES, returned(BEYOND, N_LON // 2))
    uv = lax.cond(is_polar, exchange, unused, circles)
    pairs = [
        (lon * N_LAT + lat, (lon + 1) % N_LON * N_LAT + lat)
        for lon in range(N_LON)
        for lat in range(N_LAT // 4, N_LAT - N_LAT // 4)
    ]
    west = lax.ppermute(west, AXES, pairs)
    east = lax.ppermute(east, AXES, [(j, i) for i, j in pairs])
    result = unpack(place, own_u, own_v, own_h, west, east, uv, h_first, h_second)
    return tuple(jnp.swapaxes(x.reshape(COLS, LEV, ROWS), 0, 1) for x in result)


def solution(mesh):
    placed = (P(None, "lon", "lat"),) * 3
    return jax.shard_map(shards, mesh=mesh, in_specs=placed, out_specs=placed, check_vma=False)
```

```python
import functools
import math

import jax
import jax.numpy as jnp
import numpy as np
from jax import lax
from jax.experimental import pallas as pl
from jax.experimental.pallas import tpu as pltpu
from jax.sharding import PartitionSpec as P

N_LON = 16
N_LAT = 8
LEV = 16
COLS = 180
ROWS = 128
NLON = N_LON * COLS
NLAT = N_LAT * ROWS
HALF = 192
TALL = 184
PACK = 90
CHUNK = 64
SOME = 96
AHEAD = 32
AXES = ("lon", "lat")

GRAV_ZONAL = 0.3
GRAV_MERID = 0.6
CORIOLIS = 0.8
DIVERGENCE = 0.3
DIFFUSION = 0.08


def latitude_tables():
    f32 = np.float32
    index = np.arange(NLAT).astype(f32)
    step = f32(math.pi / NLAT)

    def sine(angle):
        return np.sin(angle.astype(np.float64)).astype(f32)

    def cosine(angle):
        return np.cos(angle.astype(np.float64)).astype(f32)

    center = (index + f32(0.5)) * step
    face = (index + f32(1.0)) * step
    cos_center = sine(center)
    sin_center = -cosine(center)
    sin_face = -cosine(face)
    cos_face = np.where(index + 1 < NLAT, sine(face), f32(0.0))
    cos_south = sine(index * step)
    ratio = f32(2.0) * cos_center * cos_center
    table = np.stack(
        [
            GRAV_ZONAL / cos_center.astype(np.float64),
            CORIOLIS * 0.25 * sin_center.astype(np.float64),
            CORIOLIS * 0.25 * sin_face.astype(np.float64),
            cos_face,
            cos_south,
            ratio,
            DIVERGENCE / cos_center.astype(np.float64),
            np.zeros(NLAT),
        ]
    ).astype(f32)
    return np.ascontiguousarray(table.reshape(8, N_LAT, ROWS).transpose(1, 0, 2))


def split(value):
    high = value.astype(jnp.bfloat16)
    return high, (value - high.astype(value.dtype)).astype(jnp.bfloat16)


@functools.cache
def fourier_tables():
    at = np.arange(COLS)
    angles = (at[:, None] * at[None, :] % COLS) * (2.0 * math.pi / COLS)
    matrix = np.zeros((2, HALF, HALF), np.float32)
    matrix[0, :COLS, :COLS] = np.cos(angles)
    matrix[1, :COLS, :COLS] = np.sin(angles)
    matrix = matrix.reshape(2 * HALF, HALF)
    high = matrix.astype(jnp.bfloat16)
    low = (matrix - high.astype(np.float32)).astype(jnp.bfloat16)
    columns = np.zeros((HALF, ROWS), np.float32)
    for q in range(9):
        turn = q * at * (2.0 * math.pi / NLON)
        columns[:COLS, q] = np.cos(turn)
        columns[:COLS, 16 + q] = -np.sin(turn)
        wave = q + 16 * at
        wave = np.minimum(wave, NLON - wave)
        sine = np.sin((wave.astype(np.float32) * np.float32(math.pi / NLON)).astype(np.float64))
        sine_sq = (sine.astype(np.float32) * sine.astype(np.float32)).astype(np.float64)
        over = np.where(wave == 0, 1e30, 1.0 / np.where(wave == 0, 1.0, sine_sq))
        columns[:COLS, 32 + q] = over * scale_of(q)
    return np.concatenate([high, low], axis=0), columns


def scale_of(q):
    return (1.0 if q in (0, 8) else 2.0) / NLON


SIN = [math.sin(math.pi * t / 8) for t in range(5)]


def times(value, c, s):
    re, im = value
    return (c * re - s * im, c * im + s * re)


def forward16(x):
    e = [x[p] + x[p + 8] for p in range(8)]
    o = [x[p] - x[p + 8] for p in range(8)]
    e2 = [e[p] + e[p + 4] for p in range(4)]
    o2 = [e[p] - e[p + 4] for p in range(4)]
    a, b = e2[0] + e2[2], e2[1] + e2[3]
    pairs = [None] * 8
    pairs[0] = (a + b, a - b)
    pairs[4] = (e2[0] - e2[2], e2[3] - e2[1])
    root = SIN[2]
    u = (o2[0], -o2[2])
    w = times((o2[1], -o2[3]), root, -root)
    pairs[2] = (u[0] + w[0], u[1] + w[1])
    pairs[6] = (u[0] - w[0], w[1] - u[1])
    d = [times((o[p], -o[p + 4]), SIN[4 - p], -SIN[p]) if p else (o[p], -o[p + 4]) for p in range(4)]
    s02 = (d[0][0] + d[2][0], d[0][1] + d[2][1])
    t02 = (d[0][0] - d[2][0], d[0][1] - d[2][1])
    s13 = (d[1][0] + d[3][0], d[1][1] + d[3][1])
    t13 = (d[1][0] - d[3][0], d[1][1] - d[3][1])
    pairs[1] = (s02[0] + s13[0], s02[1] + s13[1])
    pairs[7] = (s02[0] - s13[0], s13[1] - s02[1])
    pairs[5] = (t02[0] + t13[1], t02[1] - t13[0])
    pairs[3] = (t02[0] - t13[1], -(t02[1] + t13[0]))
    return pairs


def inverse16(pairs):
    z0, z8 = pairs[0]
    a, b = z0 + z8, z0 - z8
    e2 = [a + pairs[4][0], b - pairs[4][1], a - pairs[4][0], b + pairs[4][1]]
    u, v = pairs[2], (pairs[6][0], -pairs[6][1])
    d0 = (u[0] + v[0], u[1] + v[1])
    root = SIN[2]
    d1 = times((u[0] - v[0], u[1] - v[1]), root, root)
    o2 = [d0[0], d1[0], -d0[1], -d1[1]]
    e = [e2[p] + o2[p] for p in range(4)] + [e2[p] - o2[p] for p in range(4)]
    a1, a5 = pairs[1], pairs[5]
    a9, a13 = (pairs[7][0], -pairs[7][1]), (pairs[3][0], -pairs[3][1])
    s19 = (a1[0] + a9[0], a1[1] + a9[1])
    t19 = (a1[0] - a9[0], a1[1] - a9[1])
    s5 = (a5[0] + a13[0], a5[1] + a13[1])
    t5 = (a5[0] - a13[0], a5[1] - a13[1])
    d = [
        (s19[0] + s5[0], s19[1] + s5[1]),
        (t19[0] - t5[1], t19[1] + t5[0]),
        (s19[0] - s5[0], s19[1] - s5[1]),
        (t19[0] + t5[1], t19[1] - t5[0]),
    ]
    d = [times(d[p], SIN[4 - p], SIN[p]) if p else d[p] for p in range(4)]
    o = [d[p][0] for p in range(4)] + [-d[p][1] for p in range(4)]
    return [e[p] + o[p] for p in range(8)] + [e[p] - o[p] for p in range(8)]


def row(i):
    return pl.ds(pl.multiple_of(i * LEV, LEV), LEV)


def lanes_of(shape):
    return lax.broadcasted_iota(jnp.int32, shape, len(shape) - 1)


def pack_kernel(place, h, u, v, first, second, low, high):
    step = pl.program_id(0)

    @pl.when(step == 0)
    def _():
        low[...] = jnp.zeros_like(low)
        high[...] = jnp.zeros_like(high)

    spots = [lanes_of((LEV, ROWS)) + ROWS * part for part in range(2)]
    kept_low = [[low[f, part] for part in range(2)] for f in range(3)]
    kept_high = [[high[f, part] for part in range(2)] for f in range(4)]
    for i in range(PACK):
        spot = step * PACK + i + 1
        masks = [[s == spot + k for s in spots] for k in (-1, 0, 1)]
        for f, field in enumerate((h, u, v)):
            turned = pltpu.roll(field[i * LEV : (i + 1) * LEV, :], lax.rem(spot + 1, ROWS), 1)
            for part in range(2):
                kept_high[f][part] = jnp.where(masks[1][part], turned, kept_high[f][part])
                kept_low[f][part] = jnp.where(masks[2][part], turned, kept_low[f][part])
                if f == 2:
                    kept_high[3][part] = jnp.where(masks[0][part], turned, kept_high[3][part])
    for part in range(2):
        for f in range(3):
            low[f, part] = kept_low[f][part]
        for f in range(4):
            high[f, part] = kept_high[f][part]

    @pl.when(step == pl.num_programs(0) - 1)
    def _():
        even = place[4] == 1
        for f in range(4):
            if f < 3:
                south = shift_lanes([low[f, 0], low[f, 1]], -1)
                north = [high[f, 0], high[f, 1]]
            else:
                south = [jnp.zeros((LEV, ROWS), jnp.float32)] * 2
                north = shift_lanes([high[f, 0], high[f, 1]], 1)
            for part in range(2):
                first[f, part] = jnp.where(even, north[part], south[part])
                second[f, part] = jnp.where(even, south[part], north[part])


def shift_lanes(parts, by):
    turned = [pltpu.roll(part, by % ROWS, 1) for part in parts]
    lane = lanes_of(parts[0].shape)
    fresh = lane == (0 if by > 0 else ROWS - 1)
    return [jnp.where(fresh, turned[1 - i], turned[i]) for i in range(2)]


def pack(place, height, u_wind, v_wind):
    field = pl.BlockSpec((PACK * LEV, ROWS), lambda i, s: (i, 0))
    shape = (4, 2, LEV, ROWS)
    edge = pl.BlockSpec(shape, lambda i, s: (0, 0, 0, 0))
    return pl.pallas_call(
        pack_kernel,
        grid_spec=pltpu.PrefetchScalarGridSpec(
            num_scalar_prefetch=1,
            grid=(COLS // PACK,),
            in_specs=[field, field, field],
            out_specs=[edge, edge],
            scratch_shapes=[pltpu.VMEM(shape, jnp.float32)] * 2,
        ),
        out_shape=[jax.ShapeDtypeStruct(shape, jnp.float32)] * 2,
        cost_estimate=pl.CostEstimate(flops=0, bytes_accessed=4_700_000, transcendentals=0),
    )(place, height, u_wind, v_wind)


def rim_terms(place, first, second, table, terms, beside):
    even, at_north, at_south = place[4] == 1, place[1] == 1, place[2] == 1
    lane = lanes_of((LEV, ROWS))

    def rim(f, part):
        above = jnp.where(even, first[f, part], second[f, part])
        below = jnp.where(even, second[f, part], first[f, part])
        if f == 0:
            return above, below
        turned = -second[3 if f == 2 else f, part]
        across = -second[f, part] if f == 1 else jnp.zeros_like(below)
        return jnp.where(at_north, turned, above), jnp.where(at_south, across, below)

    (h_n, h_s), (u_n, u_s), (v_n, v_s) = (
        zip(*(rim(f, part) for part in range(2))) for f in range(3)
    )
    turn_u, cos_south, diverge = (table[0, i : i + 1, 0:1] for i in (1, 4, 6))
    turn_v = table[0, 2:3, ROWS - 1 : ROWS]
    u_nw, v_se = shift_lanes(u_n, 1), shift_lanes(v_s, -1)
    for part in range(2):
        north = (
            DIFFUSION * h_n[part],
            DIFFUSION * u_n[part],
            DIFFUSION * v_n[part] - GRAV_MERID * h_n[part] - turn_v * (u_n[part] + u_nw[part]),
        )
        south = (
            DIFFUSION * h_s[part] + diverge * cos_south * v_s[part],
            DIFFUSION * u_s[part] + turn_u * (v_s[part] + v_se[part]),
            DIFFUSION * v_s[part],
        )
        for f in range(3):
            after = pltpu.roll(south[f], 1, 1)
            for odd in range(2):
                terms[f, odd, part] = jnp.where(lane % 2 == odd, north[f], after)
    last = pltpu.roll(u_n[1], (ROWS - 1 - COLS) % ROWS, 1)
    beside[0] = jnp.where(lane == ROWS - 1, -turn_v * last, 0.0)
    beside[1] = jnp.where(lane == 0, turn_u * pltpu.roll(v_s[0], ROWS - 1, 1), 0.0)


def stencil_kernel(
    polar, place, h, u, v, h_west, u_west, v_west, h_east, u_east, v_east, first, second, table,
    *refs,
):
    outs, (terms, whole, beside, sides) = refs[:-4], refs[-4:]
    step = pl.program_id(0)
    lane = lanes_of((LEV, ROWS))
    edges = (lane == 0) | (lane == ROWS - 1)

    @pl.when(step == 0)
    def _():
        rim_terms(place, first, second, table, terms, beside)

    zonal, turn_u, turn_v, cos_face, cos_south, _, diverge = (
        jnp.broadcast_to(table[0, i : i + 1, :], (LEV, ROWS)) for i in range(7)
    )

    def north(block):
        return jnp.where(lane == ROWS - 1, 0.0, pltpu.roll(block, ROWS - 1, 1))

    def south(block):
        return jnp.where(lane == 0, 0.0, pltpu.roll(block, 1, 1))

    def update(k, odd, carry, blocks_east):
        (t_west, v_south, w_here), (west_h, west_u, west_v) = carry
        mid_h, mid_u, mid_v = middle = [field[row(k), :] for field in (h, u, v)]
        east_h, east_u, east_v = blocks_east
        h_north, h_south = north(mid_h), south(mid_h)
        u_north, u_south = north(mid_u), south(mid_u)
        v_north, v_south_east = north(mid_v), south(east_v)
        t_here = mid_u + u_north
        w_east = east_v + v_south_east
        new_u = (
            mid_u
            - zonal * (east_h - mid_h)
            + turn_u * (w_here + w_east)
            + DIFFUSION * (east_u + west_u + (u_north + u_south) - 4.0 * mid_u)
        )
        new_v = (
            mid_v
            - GRAV_MERID * (h_north - mid_h)
            - turn_v * (t_here + t_west)
            + DIFFUSION * (east_v + west_v + (v_north + v_south) - 4.0 * mid_v)
        )
        new_h = (
            mid_h
            - diverge * (mid_u - west_u + cos_face * mid_v - cos_south * v_south)
            + DIFFUSION * (east_h + west_h + (h_north + h_south) - 4.0 * mid_h)
        )
        spot = step * CHUNK + k + 1
        turn = lax.rem(2 * ROWS - 1 - spot, ROWS)
        results = []
        for f, new in enumerate((new_h, new_u, new_v)):
            term = pltpu.roll(terms[f, odd, spot // ROWS], turn, 1)
            results.append(new + jnp.where(edges, term, 0.0))
        return ((t_here, v_south_east, w_east), middle), results

    def several(base, carry, beyond):
        found = []
        for n in range(AHEAD):
            k = base + n
            if n == AHEAD - 1 and beyond is not None:
                blocks = beyond
            else:
                blocks = [field[row(k + 1), :] for field in (h, u, v)]
            if n == (COLS - 1) % AHEAD:
                is_last = step * CHUNK + k == COLS - 1
                blocks = [jnp.where(is_last, 0.0, block) for block in blocks]
            carry, results = update(k, (n + 1) % 2, carry, blocks)
            found.append(results)
        for n, results in enumerate(found):
            for f in range(3):
                whole[f, row(base + n), :] = results[f]
        return carry

    before = [
        jnp.where(step == 0, 0.0, field[...]) for field in (h_west, u_west, v_west)
    ]
    here_v = v[row(0), :]
    v_south = south(here_v)
    carry = ((before[1] + north(before[1]), v_south, here_v + v_south), before)
    groups = CHUNK // AHEAD
    carry = lax.fori_loop(
        0, groups - 1, lambda c, carry: several(c * AHEAD, carry, None), carry
    )
    several((groups - 1) * AHEAD, carry, [field[...] for field in (h_east, u_east, v_east)])

    @pl.when(step == 0)
    def _():
        mid_h, mid_u, mid_v = (field[row(0), :] for field in (h, u, v))
        sides[1, 0] = DIFFUSION * mid_h
        sides[1, 1] = turn_u * (mid_v + south(mid_v)) + beside[1] - zonal * mid_h + DIFFUSION * mid_u
        sides[1, 2] = DIFFUSION * mid_v

    @pl.when(step == pl.num_programs(0) - 1)
    def _():
        end = (COLS - 1) % CHUNK
        mid_h, mid_u, mid_v = (field[row(end), :] for field in (h, u, v))
        sides[0, 0] = diverge * mid_u + DIFFUSION * mid_h
        sides[0, 1] = DIFFUSION * mid_u
        sides[0, 2] = DIFFUSION * mid_v - turn_v * (mid_u + north(mid_u)) + beside[0]
        if polar:
            for f in range(3):
                for side in range(2):
                    whole[f, row(end + 1 + side), :] = sides[side, f]

    if not polar:
        for f in range(3):
            outs[f][...] = whole[f]
        for side in range(2):
            outs[3 + side][...] = sides[side]
        return

    def turned(f):
        return jnp.transpose(whole[f].reshape(CHUNK, LEV, ROWS), (1, 0, 2))

    uv_out, h_first, h_second = outs
    height = turned(0)
    h_first[...] = height[: LEV // 2]
    h_second[...] = height[LEV // 2 :]
    uv_out[:, 0] = turned(1)
    uv_out[:, 1] = turned(2)


def stencil(polar, place, height, u_wind, v_wind, first, second, tables):
    block = pl.BlockSpec((CHUNK * LEV, ROWS), lambda i, s: (i, 0))
    one_west = pl.BlockSpec((LEV, ROWS), lambda i, s: (jnp.maximum(i * CHUNK - 1, 0), 0))
    one_east = pl.BlockSpec(
        (LEV, ROWS), lambda i, s: (jnp.minimum((i + 1) * CHUNK, COLS - 1), 0)
    )
    side = pl.BlockSpec((3, LEV, ROWS), lambda i, s: (0, 0, 0))
    edge = pl.BlockSpec((4, 2, LEV, ROWS), lambda i, s: (0, 0, 0, 0))
    sent = pl.BlockSpec((LEV // 2, CHUNK, ROWS), lambda i, s: (0, i, 0))
    pair = pl.BlockSpec((LEV, 2, CHUNK, ROWS), lambda i, s: (0, 0, i, 0))
    own = jax.ShapeDtypeStruct((COLS * LEV, ROWS), jnp.float32)
    full = jax.ShapeDtypeStruct((LEV, 2, TALL, ROWS), jnp.float32)
    half = jax.ShapeDtypeStruct((LEV // 2, TALL, ROWS), jnp.float32)
    ends = jax.ShapeDtypeStruct((3, LEV, ROWS), jnp.float32)
    fields = (height, u_wind, v_wind)
    return pl.pallas_call(
        functools.partial(stencil_kernel, polar),
        grid_spec=pltpu.PrefetchScalarGridSpec(
            num_scalar_prefetch=1,
            grid=(pl.cdiv(COLS, CHUNK),),
            in_specs=[block] * 3
            + [one_west] * 3
            + [one_east] * 3
            + [edge] * 2
            + [pl.BlockSpec((1, 8, ROWS), lambda i, s: (s[0], 0, 0))],
            out_specs=[pair, sent, sent] if polar else [block] * 3 + [side] * 2,
            scratch_shapes=[
                pltpu.VMEM((3, 2, 2, LEV, ROWS), jnp.float32),
                pltpu.VMEM((3, CHUNK * LEV, ROWS), jnp.float32),
                pltpu.VMEM((2, LEV, ROWS), jnp.float32),
                pltpu.VMEM((2, 3, LEV, ROWS), jnp.float32),
            ],
        ),
        out_shape=[full, half, half] if polar else [own] * 3 + [ends] * 2,
        compiler_params=pltpu.CompilerParams(vmem_limit_bytes=58 * 1024 * 1024),
        cost_estimate=pl.CostEstimate(
            flops=60_000_000, bytes_accessed=9_000_000, transcendentals=0
        ),
    )(place, *fields, *fields, *fields, first, second, tables)


def unpack_kernel(
    place, own_u, own_v, own_h, west, east, uv, h_first, h_second, u_out, v_out, h_out
):
    def turned(block):
        return jnp.transpose(block, (1, 0, 2)).reshape(SOME * LEV, ROWS)

    @pl.when(place[3] == 1)
    def _():
        u_out[...] = turned(uv[:, 0])
        v_out[...] = turned(uv[:, 1])
        h_out[...] = turned(jnp.concatenate([h_first[...], h_second[...]], 0))

    @pl.when(place[3] == 0)
    def _():
        u_out[...] = own_u[...]
        v_out[...] = own_v[...]
        h_out[...] = own_h[...]
        end = row((COLS - 1) % SOME)
        for f, out in enumerate((h_out, u_out, v_out)):

            @pl.when(pl.program_id(0) == 0)
            def _(f=f, out=out):
                out[row(0), :] += west[f]

            @pl.when(pl.program_id(0) == (COLS - 1) // SOME)
            def _(f=f, out=out):
                out[end, :] += east[f]


def unpack(place, own_u, own_v, own_h, west, east, uv, h_first, h_second):
    def pick(polar):
        return lambda i, s: jnp.where(s[3] == polar, i, 0)

    kept, used = pick(0), pick(1)
    half = pl.BlockSpec((LEV // 2, SOME, ROWS), lambda i, s: (0, used(i, s), 0))
    return pl.pallas_call(
        unpack_kernel,
        grid_spec=pltpu.PrefetchScalarGridSpec(
            num_scalar_prefetch=1,
            grid=(pl.cdiv(COLS, SOME),),
            in_specs=[pl.BlockSpec((SOME * LEV, ROWS), lambda i, s: (kept(i, s), 0))] * 3
            + [pl.BlockSpec((3, LEV, ROWS), lambda i, s: (0, 0, 0))] * 2
            + [pl.BlockSpec((LEV, 2, SOME, ROWS), lambda i, s: (0, 0, used(i, s), 0))]
            + [half] * 2,
            out_specs=[pl.BlockSpec((SOME * LEV, ROWS), lambda i, s: (i, 0))] * 3,
        ),
        out_shape=[jax.ShapeDtypeStruct((COLS * LEV, ROWS), jnp.float32)] * 3,
        compiler_params=pltpu.CompilerParams(vmem_limit_bytes=58 * 1024 * 1024),
        cost_estimate=pl.CostEstimate(
            flops=0, bytes_accessed=24 * COLS * LEV * ROWS, transcendentals=0
        ),
    )(place, own_u, own_v, own_h, west, east, uv, h_first, h_second)


def filter_kernel(place, x, matrix, columns, table, out, spectra, waves):
    def column(rows, q):
        return columns[rows, q : q + 1]

    def gather(start, blocks):
        rows = pl.ds(pl.multiple_of(start, 16), 16)
        pairs = forward16(blocks)
        parts = [(pairs[0][0], None)] + pairs[1:] + [(pairs[0][1], None)]
        for q, (re, im) in enumerate(parts):
            if q == 0:
                im = jnp.zeros_like(re)
            else:
                c, s = column(rows, q), column(rows, 16 + q)
                re, im = (c * re, s * re) if im is None else times((re, im), c, s)
            for side, value in enumerate((re, im)):
                high, low = split(value)
                spectra[q, 0, rows, side * ROWS : (side + 1) * ROWS] = high
                spectra[q, 1, rows, side * ROWS : (side + 1) * ROWS] = low

    at = lax.broadcasted_iota(jnp.int32, (16, ROWS), 0)

    def with_beside(blocks, spot, source, distance):
        return [
            block + jnp.where(at == spot, x[(p + distance) % 16, source : source + 1, :], 0.0)
            for p, block in enumerate(blocks)
        ]

    gather(0, with_beside([x[p, 0:16, :] for p in range(16)], 0, COLS, -1))

    def fill(c, carry):
        start = pl.multiple_of(c * 16, 16)
        gather(start, [x[p, pl.ds(start, 16), :] for p in range(16)])
        return carry

    full = COLS // 16
    lax.fori_loop(1, full, fill, 0, unroll=full - 1)
    empty = jnp.zeros((HALF - COLS, ROWS), jnp.float32)
    tail = pl.ds(16 * full, COLS % 16)
    blocks = [jnp.concatenate([x[p, tail, :], empty], 0) for p in range(16)]
    gather(16 * full, with_beside(blocks, COLS % 16 - 1, COLS + 1, 1))

    def product(high, low):
        found = jnp.dot(matrix[: 2 * HALF], high, preferred_element_type=jnp.float32)
        found += jnp.dot(matrix[2 * HALF :], high, preferred_element_type=jnp.float32)
        found += jnp.dot(matrix[: 2 * HALF], low, preferred_element_type=jnp.float32)
        cos, sin = found[:HALF], found[HALF:]
        return cos[:, :ROWS], cos[:, ROWS:], sin[:, :ROWS], sin[:, ROWS:]

    ratio = table[0, 5:6, :]
    rows = slice(0, HALF)
    for q in range(9):
        cos_re, cos_im, sin_re, sin_im = product(spectra[q, 0], spectra[q, 1])
        damping = jnp.minimum(ratio * column(rows, 32 + q), scale_of(q))
        re, im = damping * (cos_re + sin_im), damping * (cos_im - sin_re)
        cos_re, cos_im, sin_re, sin_im = product(*split(jnp.concatenate([re, im], 1)))
        re = cos_re - sin_im
        if q:
            im = cos_im + sin_re
            c, s = column(rows, q), column(rows, 16 + q)
            if q < 8:
                waves[q, 1] = c * im - s * re
            re = c * re + s * im
        waves[q, 0] = re

    def give(c, carry):
        rows = pl.ds(pl.multiple_of(c * 8, 8), 8)
        pairs = [(waves[0, 0, rows, :], waves[8, 0, rows, :])]
        pairs += [(waves[q, 0, rows, :], waves[q, 1, rows, :]) for q in range(1, 8)]
        for p, value in enumerate(inverse16(pairs)):
            out[p, rows, :] = value
        return carry

    lax.fori_loop(0, TALL // 8, give, 0, unroll=TALL // 8)


def polar_filter(place, x, tables):
    matrix, columns = fourier_tables()
    field = pl.BlockSpec((LEV, None, TALL, ROWS), lambda i, s: (0, i, 0, 0))
    return pl.pallas_call(
        filter_kernel,
        grid_spec=pltpu.PrefetchScalarGridSpec(
            num_scalar_prefetch=1,
            grid=(x.shape[1],),
            in_specs=[
                field,
                pl.BlockSpec(matrix.shape, lambda i, s: (0, 0)),
                pl.BlockSpec(columns.shape, lambda i, s: (0, 0)),
                pl.BlockSpec((1, 8, ROWS), lambda i, s: (s[0], 0, 0)),
            ],
            out_specs=field,
            scratch_shapes=[
                pltpu.VMEM((9, 2, HALF, 2 * ROWS), jnp.bfloat16),
                pltpu.VMEM((9, 2, HALF, ROWS), jnp.float32),
            ],
        ),
        out_shape=jax.ShapeDtypeStruct(x.shape, jnp.float32),
        compiler_params=pltpu.CompilerParams(vmem_limit_bytes=28 * 1024 * 1024),
        cost_estimate=pl.CostEstimate(
            flops=216 * HALF * HALF * ROWS * x.shape[1], bytes_accessed=3_500_000 * x.shape[1], transcendentals=0
        ),
    )(place, x, jnp.asarray(matrix), jnp.asarray(columns), tables)


BESIDE = ((0, 3), (1, 2), (6, 5), (7, 4))
BEYOND = ((0, 4), (1, 5), (6, 2), (7, 3))


def lent(pairs, turn):
    return [
        (lon * N_LAT + polar, (lon ^ turn) * N_LAT + other)
        for lon in range(N_LON)
        for polar, other in pairs
    ]


def returned(pairs, turn):
    return [(j, i) for i, j in lent(pairs, turn)]


def partner(band, pairs):
    return sum(jnp.where(band == other, polar, 0) for polar, other in pairs).astype(jnp.int32)


def unused(*likes):
    return pl.pallas_call(
        lambda *outs: None,
        out_specs=[pl.BlockSpec(memory_space=pl.ANY)] * len(likes),
        out_shape=[jax.ShapeDtypeStruct(like.shape, like.dtype) for like in likes],
    )()


def shards(u_wind, v_wind, height):
    band = lax.axis_index("lat")
    is_polar = (band < N_LAT // 4) | (band >= N_LAT - N_LAT // 4)
    even = band % 2 == 0
    place = jnp.stack([band, band == N_LAT - 1, band == 0, is_polar, even]).astype(jnp.int32)
    tables = jnp.asarray(latitude_tables())
    fields = [jnp.swapaxes(x, 0, 1) for x in (height, u_wind, v_wind)]
    flat = [x.reshape(COLS * LEV, ROWS) for x in fields]
    first, second = pack(place, *flat)
    swap = [(i, i ^ 1) for i in range(N_LAT)]
    first = lax.ppermute(first, "lat", swap)
    routes = [(lon, i, lon, i + 1) for lon in range(N_LON) for i in range(1, N_LAT - 1, 2)]
    routes += [(lon, i + 1, lon, i) for lon, i, _, _ in routes]
    routes += [
        (lon, i, (lon + N_LON // 2) % N_LON, i) for lon in range(N_LON) for i in (0, N_LAT - 1)
    ]
    second = lax.ppermute(
        second,
        AXES,
        [(a * N_LAT + b, c * N_LAT + d) for a, b, c, d in routes],
    )
    def exchange(value):
        return lax.all_to_all(value, "lon", split_axis=0, concat_axis=0, tiled=True)

    def help_out(h_first, h_second):
        circles = exchange(jnp.concatenate([h_first, h_second], 0))
        lender = jnp.where(
            lax.axis_index("lon") < N_LON // 2, partner(band, BESIDE), partner(band, BEYOND)
        )
        smooth = polar_filter(lender.reshape(1), circles[:, None], tables)[:, 0]
        h = exchange(smooth)
        return h[: LEV // 2], h[LEV // 2 :]

    inputs = (place, *flat, first, second, tables)
    whole = jax.ShapeDtypeStruct((LEV, 2, TALL, ROWS), jnp.float32)
    half = jax.ShapeDtypeStruct((LEV // 2, TALL, ROWS), jnp.float32)
    own = jax.ShapeDtypeStruct((COLS * LEV, ROWS), jnp.float32)
    ends = jax.ShapeDtypeStruct((3, LEV, ROWS), jnp.float32)
    uv, h_first, h_second = lax.cond(
        is_polar,
        lambda *inputs: tuple(stencil(True, *inputs)),
        lambda *inputs: tuple(unused(whole, half, half)),
        *inputs,
    )

    h_first = lax.ppermute(h_first, AXES, lent(BESIDE, 0))
    h_second = lax.ppermute(h_second, AXES, lent(BEYOND, N_LON // 2))
    def beside(own_h, own_u, own_v, onward, back):
        me = lax.axis_index("lon")
        to = jnp.arange(N_LON).reshape(N_LON, 1, 1, 1)
        sent = jnp.where(to == (me + 1) % N_LON, onward, 0.0)
        got = exchange(jnp.where(to == (me - 1) % N_LON, back, sent))

        def of(source):
            return lax.dynamic_index_in_dim(got, source % N_LON, 0, keepdims=False)

        return own_h, own_u, own_v, of(me - 1), of(me + 1)

    circles, own_h, own_u, own_v, west, east = lax.cond(
        is_polar,
        lambda uv, *inputs: (
            polar_filter(place, exchange(uv), tables),
            *unused(own, own, own, ends, ends),
        ),
        lambda uv, *inputs: (*unused(uv), *beside(*stencil(False, *inputs))),
        uv, *inputs,
    )
    h_first, h_second, circles = lax.optimization_barrier((h_first, h_second, circles))
    h_first, h_second = lax.cond(
        is_polar, lambda *parts: tuple(unused(*parts)), help_out, h_first, h_second
    )
    h_first = lax.ppermute(h_first, AXES, returned(BESIDE, 0))
    h_second = lax.ppermute(h_second, AXES, returned(BEYOND, N_LON // 2))
    uv = lax.cond(is_polar, exchange, lambda like: unused(like)[0], circles)
    result = unpack(place, own_u, own_v, own_h, west, east, uv, h_first, h_second)
    return tuple(jnp.swapaxes(x.reshape(COLS, LEV, ROWS), 0, 1) for x in result)


def solution(mesh):
    placed = (P(None, "lon", "lat"),) * 3
    return jax.shard_map(shards, mesh=mesh, in_specs=placed, out_specs=placed, check_vma=False)
```

```python
import functools
import math

import jax
import jax.numpy as jnp
import numpy as np
from jax import lax
from jax.experimental import pallas as pl
from jax.experimental.pallas import tpu as pltpu
from jax.sharding import PartitionSpec as P

N_LON = 16
N_LAT = 8
LEV = 16
COLS = 180
ROWS = 128
NLON = N_LON * COLS
NLAT = N_LAT * ROWS
HALF = 192
TALL = 184
PACK = 90
CHUNK = 64
SOME = 96
AHEAD = 32
AXES = ("lon", "lat")

GRAV_ZONAL = 0.3
GRAV_MERID = 0.6
CORIOLIS = 0.8
DIVERGENCE = 0.3
DIFFUSION = 0.08


def latitude_tables():
    f32 = np.float32
    index = np.arange(NLAT).astype(f32)
    step = f32(math.pi / NLAT)

    def sine(angle):
        return np.sin(angle.astype(np.float64)).astype(f32)

    def cosine(angle):
        return np.cos(angle.astype(np.float64)).astype(f32)

    center = (index + f32(0.5)) * step
    face = (index + f32(1.0)) * step
    cos_center = sine(center)
    sin_center = -cosine(center)
    sin_face = -cosine(face)
    cos_face = np.where(index + 1 < NLAT, sine(face), f32(0.0))
    cos_south = sine(index * step)
    ratio = f32(2.0) * cos_center * cos_center
    table = np.stack(
        [
            GRAV_ZONAL / cos_center.astype(np.float64),
            CORIOLIS * 0.25 * sin_center.astype(np.float64),
            CORIOLIS * 0.25 * sin_face.astype(np.float64),
            cos_face,
            cos_south,
            ratio,
            DIVERGENCE / cos_center.astype(np.float64),
            np.zeros(NLAT),
        ]
    ).astype(f32)
    return np.ascontiguousarray(table.reshape(8, N_LAT, ROWS).transpose(1, 0, 2))


def split(value):
    high = value.astype(jnp.bfloat16)
    return high, (value - high.astype(value.dtype)).astype(jnp.bfloat16)


@functools.cache
def fourier_tables():
    at = np.arange(COLS)
    angles = (at[:, None] * at[None, :] % COLS) * (2.0 * math.pi / COLS)
    matrix = np.zeros((2, HALF, HALF), np.float32)
    matrix[0, :COLS, :COLS] = np.cos(angles)
    matrix[1, :COLS, :COLS] = np.sin(angles)
    matrix = matrix.reshape(2 * HALF, HALF)
    high = matrix.astype(jnp.bfloat16)
    low = (matrix - high.astype(np.float32)).astype(jnp.bfloat16)
    columns = np.zeros((HALF, ROWS), np.float32)
    for q in range(9):
        turn = q * at * (2.0 * math.pi / NLON)
        columns[:COLS, q] = np.cos(turn)
        columns[:COLS, 16 + q] = -np.sin(turn)
        wave = q + 16 * at
        wave = np.minimum(wave, NLON - wave)
        sine = np.sin((wave.astype(np.float32) * np.float32(math.pi / NLON)).astype(np.float64))
        sine_sq = (sine.astype(np.float32) * sine.astype(np.float32)).astype(np.float64)
        over = np.where(wave == 0, 1e30, 1.0 / np.where(wave == 0, 1.0, sine_sq))
        columns[:COLS, 32 + q] = over * scale_of(q)
    return np.concatenate([high, low], axis=0), columns


def scale_of(q):
    return (1.0 if q in (0, 8) else 2.0) / NLON


SIN = [math.sin(math.pi * t / 8) for t in range(5)]


def times(value, c, s):
    re, im = value
    return (c * re - s * im, c * im + s * re)


def forward16(x):
    e = [x[p] + x[p + 8] for p in range(8)]
    o = [x[p] - x[p + 8] for p in range(8)]
    e2 = [e[p] + e[p + 4] for p in range(4)]
    o2 = [e[p] - e[p + 4] for p in range(4)]
    a, b = e2[0] + e2[2], e2[1] + e2[3]
    pairs = [None] * 8
    pairs[0] = (a + b, a - b)
    pairs[4] = (e2[0] - e2[2], e2[3] - e2[1])
    root = SIN[2]
    u = (o2[0], -o2[2])
    w = times((o2[1], -o2[3]), root, -root)
    pairs[2] = (u[0] + w[0], u[1] + w[1])
    pairs[6] = (u[0] - w[0], w[1] - u[1])
    d = [times((o[p], -o[p + 4]), SIN[4 - p], -SIN[p]) if p else (o[p], -o[p + 4]) for p in range(4)]
    s02 = (d[0][0] + d[2][0], d[0][1] + d[2][1])
    t02 = (d[0][0] - d[2][0], d[0][1] - d[2][1])
    s13 = (d[1][0] + d[3][0], d[1][1] + d[3][1])
    t13 = (d[1][0] - d[3][0], d[1][1] - d[3][1])
    pairs[1] = (s02[0] + s13[0], s02[1] + s13[1])
    pairs[7] = (s02[0] - s13[0], s13[1] - s02[1])
    pairs[5] = (t02[0] + t13[1], t02[1] - t13[0])
    pairs[3] = (t02[0] - t13[1], -(t02[1] + t13[0]))
    return pairs


def inverse16(pairs):
    z0, z8 = pairs[0]
    a, b = z0 + z8, z0 - z8
    e2 = [a + pairs[4][0], b - pairs[4][1], a - pairs[4][0], b + pairs[4][1]]
    u, v = pairs[2], (pairs[6][0], -pairs[6][1])
    d0 = (u[0] + v[0], u[1] + v[1])
    root = SIN[2]
    d1 = times((u[0] - v[0], u[1] - v[1]), root, root)
    o2 = [d0[0], d1[0], -d0[1], -d1[1]]
    e = [e2[p] + o2[p] for p in range(4)] + [e2[p] - o2[p] for p in range(4)]
    a1, a5 = pairs[1], pairs[5]
    a9, a13 = (pairs[7][0], -pairs[7][1]), (pairs[3][0], -pairs[3][1])
    s19 = (a1[0] + a9[0], a1[1] + a9[1])
    t19 = (a1[0] - a9[0], a1[1] - a9[1])
    s5 = (a5[0] + a13[0], a5[1] + a13[1])
    t5 = (a5[0] - a13[0], a5[1] - a13[1])
    d = [
        (s19[0] + s5[0], s19[1] + s5[1]),
        (t19[0] - t5[1], t19[1] + t5[0]),
        (s19[0] - s5[0], s19[1] - s5[1]),
        (t19[0] + t5[1], t19[1] - t5[0]),
    ]
    d = [times(d[p], SIN[4 - p], SIN[p]) if p else d[p] for p in range(4)]
    o = [d[p][0] for p in range(4)] + [-d[p][1] for p in range(4)]
    return [e[p] + o[p] for p in range(8)] + [e[p] - o[p] for p in range(8)]


def row(i):
    return pl.ds(pl.multiple_of(i * LEV, LEV), LEV)


def lanes_of(shape):
    return lax.broadcasted_iota(jnp.int32, shape, len(shape) - 1)


def pack_kernel(place, h, u, v, first, second, low, high):
    step = pl.program_id(0)

    @pl.when(step == 0)
    def _():
        low[...] = jnp.zeros_like(low)
        high[...] = jnp.zeros_like(high)

    spots = [lanes_of((LEV, ROWS)) + ROWS * part for part in range(2)]
    kept_low = [[low[f, part] for part in range(2)] for f in range(3)]
    kept_high = [[high[f, part] for part in range(2)] for f in range(4)]
    for i in range(PACK):
        spot = step * PACK + i + 1
        masks = [[s == spot + k for s in spots] for k in (-1, 0, 1)]
        for f, field in enumerate((h, u, v)):
            turned = pltpu.roll(field[i * LEV : (i + 1) * LEV, :], lax.rem(spot + 1, ROWS), 1)
            for part in range(2):
                kept_high[f][part] = jnp.where(masks[1][part], turned, kept_high[f][part])
                kept_low[f][part] = jnp.where(masks[2][part], turned, kept_low[f][part])
                if f == 2:
                    kept_high[3][part] = jnp.where(masks[0][part], turned, kept_high[3][part])
    for part in range(2):
        for f in range(3):
            low[f, part] = kept_low[f][part]
        for f in range(4):
            high[f, part] = kept_high[f][part]

    @pl.when(step == pl.num_programs(0) - 1)
    def _():
        even = place[4] == 1
        for f in range(4):
            if f < 3:
                south = shift_lanes([low[f, 0], low[f, 1]], -1)
                north = [high[f, 0], high[f, 1]]
            else:
                south = [jnp.zeros((LEV, ROWS), jnp.float32)] * 2
                north = shift_lanes([high[f, 0], high[f, 1]], 1)
            for part in range(2):
                first[f, part] = jnp.where(even, north[part], south[part])
                second[f, part] = jnp.where(even, south[part], north[part])


def shift_lanes(parts, by):
    turned = [pltpu.roll(part, by % ROWS, 1) for part in parts]
    lane = lanes_of(parts[0].shape)
    fresh = lane == (0 if by > 0 else ROWS - 1)
    return [jnp.where(fresh, turned[1 - i], turned[i]) for i in range(2)]


def pack(place, height, u_wind, v_wind):
    field = pl.BlockSpec((PACK * LEV, ROWS), lambda i, s: (i, 0))
    shape = (4, 2, LEV, ROWS)
    edge = pl.BlockSpec(shape, lambda i, s: (0, 0, 0, 0))
    return pl.pallas_call(
        pack_kernel,
        grid_spec=pltpu.PrefetchScalarGridSpec(
            num_scalar_prefetch=1,
            grid=(COLS // PACK,),
            in_specs=[field, field, field],
            out_specs=[edge, edge],
            scratch_shapes=[pltpu.VMEM(shape, jnp.float32)] * 2,
        ),
        out_shape=[jax.ShapeDtypeStruct(shape, jnp.float32)] * 2,
        cost_estimate=pl.CostEstimate(flops=0, bytes_accessed=4_700_000, transcendentals=0),
    )(place, height, u_wind, v_wind)


def rim_terms(place, first, second, table, terms, beside):
    even, at_north, at_south = place[4] == 1, place[1] == 1, place[2] == 1
    lane = lanes_of((LEV, ROWS))

    def rim(f, part):
        above = jnp.where(even, first[f, part], second[f, part])
        below = jnp.where(even, second[f, part], first[f, part])
        if f == 0:
            return above, below
        turned = -second[3 if f == 2 else f, part]
        across = -second[f, part] if f == 1 else jnp.zeros_like(below)
        return jnp.where(at_north, turned, above), jnp.where(at_south, across, below)

    (h_n, h_s), (u_n, u_s), (v_n, v_s) = (
        zip(*(rim(f, part) for part in range(2))) for f in range(3)
    )
    turn_u, cos_south, diverge = (table[0, i : i + 1, 0:1] for i in (1, 4, 6))
    turn_v = table[0, 2:3, ROWS - 1 : ROWS]
    u_nw, v_se = shift_lanes(u_n, 1), shift_lanes(v_s, -1)
    for part in range(2):
        north = (
            DIFFUSION * h_n[part],
            DIFFUSION * u_n[part],
            DIFFUSION * v_n[part] - GRAV_MERID * h_n[part] - turn_v * (u_n[part] + u_nw[part]),
        )
        south = (
            DIFFUSION * h_s[part] + diverge * cos_south * v_s[part],
            DIFFUSION * u_s[part] + turn_u * (v_s[part] + v_se[part]),
            DIFFUSION * v_s[part],
        )
        for f in range(3):
            after = pltpu.roll(south[f], 1, 1)
            for odd in range(2):
                terms[f, odd, part] = jnp.where(lane % 2 == odd, north[f], after)
    last = pltpu.roll(u_n[1], (ROWS - 1 - COLS) % ROWS, 1)
    beside[0] = jnp.where(lane == ROWS - 1, -turn_v * last, 0.0)
    beside[1] = jnp.where(lane == 0, turn_u * pltpu.roll(v_s[0], ROWS - 1, 1), 0.0)


def stencil_kernel(
    polar, place, h, u, v, h_west, u_west, v_west, h_east, u_east, v_east, first, second, table,
    *refs,
):
    outs, (terms, whole, beside, sides) = refs[:-4], refs[-4:]
    step = pl.program_id(0)
    lane = lanes_of((LEV, ROWS))
    edges = (lane == 0) | (lane == ROWS - 1)

    @pl.when(step == 0)
    def _():
        rim_terms(place, first, second, table, terms, beside)

    zonal, turn_u, turn_v, cos_face, cos_south, _, diverge = (
        jnp.broadcast_to(table[0, i : i + 1, :], (LEV, ROWS)) for i in range(7)
    )

    def north(block):
        return jnp.where(lane == ROWS - 1, 0.0, pltpu.roll(block, ROWS - 1, 1))

    def south(block):
        return jnp.where(lane == 0, 0.0, pltpu.roll(block, 1, 1))

    def update(k, odd, carry, blocks_east):
        (t_west, v_south, w_here), (west_h, west_u, west_v) = carry
        mid_h, mid_u, mid_v = middle = [field[row(k), :] for field in (h, u, v)]
        east_h, east_u, east_v = blocks_east
        h_north, h_south = north(mid_h), south(mid_h)
        u_north, u_south = north(mid_u), south(mid_u)
        v_north, v_south_east = north(mid_v), south(east_v)
        t_here = mid_u + u_north
        w_east = east_v + v_south_east
        new_u = (
            mid_u
            - zonal * (east_h - mid_h)
            + turn_u * (w_here + w_east)
            + DIFFUSION * (east_u + west_u + (u_north + u_south) - 4.0 * mid_u)
        )
        new_v = (
            mid_v
            - GRAV_MERID * (h_north - mid_h)
            - turn_v * (t_here + t_west)
            + DIFFUSION * (east_v + west_v + (v_north + v_south) - 4.0 * mid_v)
        )
        new_h = (
            mid_h
            - diverge * (mid_u - west_u + cos_face * mid_v - cos_south * v_south)
            + DIFFUSION * (east_h + west_h + (h_north + h_south) - 4.0 * mid_h)
        )
        spot = step * CHUNK + k + 1
        turn = lax.rem(2 * ROWS - 1 - spot, ROWS)
        results = []
        for f, new in enumerate((new_h, new_u, new_v)):
            term = pltpu.roll(terms[f, odd, spot // ROWS], turn, 1)
            results.append(new + jnp.where(edges, term, 0.0))
        return ((t_here, v_south_east, w_east), middle), results

    def several(base, carry, beyond):
        found = []
        for n in range(AHEAD):
            k = base + n
            if n == AHEAD - 1 and beyond is not None:
                blocks = beyond
            else:
                blocks = [field[row(k + 1), :] for field in (h, u, v)]
            if n == (COLS - 1) % AHEAD:
                is_last = step * CHUNK + k == COLS - 1
                blocks = [jnp.where(is_last, 0.0, block) for block in blocks]
            carry, results = update(k, (n + 1) % 2, carry, blocks)
            found.append(results)
        for n, results in enumerate(found):
            for f in range(3):
                whole[f, row(base + n), :] = results[f]
        return carry

    before = [
        jnp.where(step == 0, 0.0, field[...]) for field in (h_west, u_west, v_west)
    ]
    here_v = v[row(0), :]
    v_south = south(here_v)
    carry = ((before[1] + north(before[1]), v_south, here_v + v_south), before)
    groups = CHUNK // AHEAD
    carry = lax.fori_loop(
        0, groups - 1, lambda c, carry: several(c * AHEAD, carry, None), carry
    )
    several((groups - 1) * AHEAD, carry, [field[...] for field in (h_east, u_east, v_east)])

    @pl.when(step == 0)
    def _():
        mid_h, mid_u, mid_v = (field[row(0), :] for field in (h, u, v))
        sides[1, 0] = DIFFUSION * mid_h
        sides[1, 1] = turn_u * (mid_v + south(mid_v)) + beside[1] - zonal * mid_h + DIFFUSION * mid_u
        sides[1, 2] = DIFFUSION * mid_v

    @pl.when(step == pl.num_programs(0) - 1)
    def _():
        end = (COLS - 1) % CHUNK
        mid_h, mid_u, mid_v = (field[row(end), :] for field in (h, u, v))
        sides[0, 0] = diverge * mid_u + DIFFUSION * mid_h
        sides[0, 1] = DIFFUSION * mid_u
        sides[0, 2] = DIFFUSION * mid_v - turn_v * (mid_u + north(mid_u)) + beside[0]
        if polar:
            for f in range(3):
                for side in range(2):
                    whole[f, row(end + 1 + side), :] = sides[side, f]

    if not polar:
        for f in range(3):
            outs[f][...] = whole[f]
        for side in range(2):
            outs[3 + side][...] = sides[side]
        return

    def turned(f):
        return jnp.transpose(whole[f].reshape(CHUNK, LEV, ROWS), (1, 0, 2))

    uv_out, h_first, h_second = outs
    height = turned(0)
    h_first[...] = height[: LEV // 2]
    h_second[...] = height[LEV // 2 :]
    uv_out[:, 0] = turned(1)
    uv_out[:, 1] = turned(2)


def stencil(polar, place, height, u_wind, v_wind, first, second, tables):
    block = pl.BlockSpec((CHUNK * LEV, ROWS), lambda i, s: (i, 0))
    one_west = pl.BlockSpec((LEV, ROWS), lambda i, s: (jnp.maximum(i * CHUNK - 1, 0), 0))
    one_east = pl.BlockSpec(
        (LEV, ROWS), lambda i, s: (jnp.minimum((i + 1) * CHUNK, COLS - 1), 0)
    )
    side = pl.BlockSpec((3, LEV, ROWS), lambda i, s: (0, 0, 0))
    edge = pl.BlockSpec((4, 2, LEV, ROWS), lambda i, s: (0, 0, 0, 0))
    sent = pl.BlockSpec((LEV // 2, CHUNK, ROWS), lambda i, s: (0, i, 0))
    pair = pl.BlockSpec((LEV, 2, CHUNK, ROWS), lambda i, s: (0, 0, i, 0))
    own = jax.ShapeDtypeStruct((COLS * LEV, ROWS), jnp.float32)
    full = jax.ShapeDtypeStruct((LEV, 2, TALL, ROWS), jnp.float32)
    half = jax.ShapeDtypeStruct((LEV // 2, TALL, ROWS), jnp.float32)
    ends = jax.ShapeDtypeStruct((3, LEV, ROWS), jnp.float32)
    fields = (height, u_wind, v_wind)
    return pl.pallas_call(
        functools.partial(stencil_kernel, polar),
        grid_spec=pltpu.PrefetchScalarGridSpec(
            num_scalar_prefetch=1,
            grid=(pl.cdiv(COLS, CHUNK),),
            in_specs=[block] * 3
            + [one_west] * 3
            + [one_east] * 3
            + [edge] * 2
            + [pl.BlockSpec((1, 8, ROWS), lambda i, s: (s[0], 0, 0))],
            out_specs=[pair, sent, sent] if polar else [block] * 3 + [side] * 2,
            scratch_shapes=[
                pltpu.VMEM((3, 2, 2, LEV, ROWS), jnp.float32),
                pltpu.VMEM((3, CHUNK * LEV, ROWS), jnp.float32),
                pltpu.VMEM((2, LEV, ROWS), jnp.float32),
                pltpu.VMEM((2, 3, LEV, ROWS), jnp.float32),
            ],
        ),
        out_shape=[full, half, half] if polar else [own] * 3 + [ends] * 2,
        compiler_params=pltpu.CompilerParams(vmem_limit_bytes=58 * 1024 * 1024),
        cost_estimate=pl.CostEstimate(
            flops=60_000_000, bytes_accessed=9_000_000, transcendentals=0
        ),
    )(place, *fields, *fields, *fields, first, second, tables)


def unpack_kernel(
    place, own_u, own_v, own_h, west, east, uv, h_first, h_second, u_out, v_out, h_out
):
    def turned(block):
        return jnp.transpose(block, (1, 0, 2)).reshape(SOME * LEV, ROWS)

    @pl.when(place[3] == 1)
    def _():
        u_out[...] = turned(uv[:, 0])
        v_out[...] = turned(uv[:, 1])
        h_out[...] = turned(jnp.concatenate([h_first[...], h_second[...]], 0))

    @pl.when(place[3] == 0)
    def _():
        u_out[...] = own_u[...]
        v_out[...] = own_v[...]
        h_out[...] = own_h[...]
        end = row((COLS - 1) % SOME)
        for f, out in enumerate((h_out, u_out, v_out)):

            @pl.when(pl.program_id(0) == 0)
            def _(f=f, out=out):
                out[row(0), :] += west[f]

            @pl.when(pl.program_id(0) == (COLS - 1) // SOME)
            def _(f=f, out=out):
                out[end, :] += east[f]


def unpack(place, own_u, own_v, own_h, west, east, uv, h_first, h_second):
    def pick(polar):
        return lambda i, s: jnp.where(s[3] == polar, i, 0)

    kept, used = pick(0), pick(1)
    half = pl.BlockSpec((LEV // 2, SOME, ROWS), lambda i, s: (0, used(i, s), 0))
    return pl.pallas_call(
        unpack_kernel,
        grid_spec=pltpu.PrefetchScalarGridSpec(
            num_scalar_prefetch=1,
            grid=(pl.cdiv(COLS, SOME),),
            in_specs=[pl.BlockSpec((SOME * LEV, ROWS), lambda i, s: (kept(i, s), 0))] * 3
            + [pl.BlockSpec((3, LEV, ROWS), lambda i, s: (0, 0, 0))] * 2
            + [pl.BlockSpec((LEV, 2, SOME, ROWS), lambda i, s: (0, 0, used(i, s), 0))]
            + [half] * 2,
            out_specs=[pl.BlockSpec((SOME * LEV, ROWS), lambda i, s: (i, 0))] * 3,
        ),
        out_shape=[jax.ShapeDtypeStruct((COLS * LEV, ROWS), jnp.float32)] * 3,
        compiler_params=pltpu.CompilerParams(vmem_limit_bytes=58 * 1024 * 1024),
        cost_estimate=pl.CostEstimate(
            flops=0, bytes_accessed=24 * COLS * LEV * ROWS, transcendentals=0
        ),
    )(place, own_u, own_v, own_h, west, east, uv, h_first, h_second)


def filter_kernel(place, x, matrix, columns, table, result, out, spectra, waves, done):
    at = lax.broadcasted_iota(jnp.int32, (16, ROWS), 0)
    full = COLS // 16
    empty = jnp.zeros((HALF - COLS, ROWS), jnp.float32)
    ratio = table[0, 5:6, :]

    def column(rows, q):
        return columns[rows, q : q + 1]

    def gather(item, c):
        rows = slice(c * 16, c * 16 + 16)
        if c < full:
            blocks = [x[p, item, rows, :] for p in range(16)]
        else:
            tail = slice(c * 16, COLS)
            blocks = [jnp.concatenate([x[p, item, tail, :], empty], 0) for p in range(16)]
        for chunk, spot, source, distance in ((0, 0, COLS, -1), (full, COLS % 16 - 1, COLS + 1, 1)):
            if c == chunk:
                blocks = [
                    block
                    + jnp.where(
                        at == spot, x[(p + distance) % 16, item, source : source + 1, :], 0.0
                    )
                    for p, block in enumerate(blocks)
                ]
        pairs = forward16(blocks)
        parts = [(pairs[0][0], None)] + pairs[1:] + [(pairs[0][1], None)]
        for q, (re, im) in enumerate(parts):
            if q == 0:
                im = jnp.zeros_like(re)
            else:
                c, s = column(rows, q), column(rows, 16 + q)
                re, im = (c * re, s * re) if im is None else times((re, im), c, s)
            for side, value in enumerate((re, im)):
                high, low = split(value)
                spectra[item, q, 0, rows, side * ROWS : (side + 1) * ROWS] = high
                spectra[item, q, 1, rows, side * ROWS : (side + 1) * ROWS] = low

    def product(high, low):
        found = jnp.dot(matrix[: 2 * HALF], high, preferred_element_type=jnp.float32)
        found += jnp.dot(matrix[2 * HALF :], high, preferred_element_type=jnp.float32)
        found += jnp.dot(matrix[: 2 * HALF], low, preferred_element_type=jnp.float32)
        cos, sin = found[:HALF], found[HALF:]
        return cos[:, :ROWS], cos[:, ROWS:], sin[:, :ROWS], sin[:, ROWS:]

    def damp(item, q):
        rows = slice(0, HALF)
        cos_re, cos_im, sin_re, sin_im = product(spectra[item, q, 0], spectra[item, q, 1])
        damping = jnp.minimum(ratio * column(rows, 32 + q), scale_of(q))
        re, im = damping * (cos_re + sin_im), damping * (cos_im - sin_re)
        cos_re, cos_im, sin_re, sin_im = product(*split(jnp.concatenate([re, im], 1)))
        re = cos_re - sin_im
        if q:
            im = cos_im + sin_re
            c, s = column(rows, q), column(rows, 16 + q)
            if q < 8:
                waves[item, q, 1] = c * im - s * re
            re = c * re + s * im
        waves[item, q, 0] = re

    def give(item, c):
        rows = slice(c * 8, c * 8 + 8)
        pairs = [(waves[item, 0, 0, rows, :], waves[item, 8, 0, rows, :])]
        pairs += [(waves[item, q, 0, rows, :], waves[item, q, 1, rows, :]) for q in range(1, 8)]
        for p, value in enumerate(inverse16(pairs)):
            out[p, item, rows, :] = value

    items = x.shape[1]
    gathers, gives = HALF // 16, TALL // 8
    copies = []

    def send(item, first, count):
        rows = pl.ds(first, count)
        copies.append(
            pltpu.make_async_copy(
                out.at[:, item, rows, :], result.at[:, item, rows, :], done.at[len(copies)]
            )
        )
        copies[-1].start()

    for c in range(gathers):
        gather(0, c)
    for item in range(items):
        for q in range(9):
            damp(item, q)
            if item + 1 < items:
                for c in range(q * gathers // 9, (q + 1) * gathers // 9):
                    gather(item + 1, c)
            if item:
                for c in range(q * gives // 9, (q + 1) * gives // 9):
                    give(item - 1, c)
        if item:
            send(item - 1, 0, TALL)
    for c in range(gives):
        give(items - 1, c)
        if c == 11:
            send(items - 1, 0, 96)
    send(items - 1, 96, TALL - 96)
    for copy in copies:
        copy.wait()


def polar_filter(place, x, tables):
    matrix, columns = fourier_tables()
    items = x.shape[1]
    vmem = pl.BlockSpec(memory_space=pltpu.VMEM)
    return pl.pallas_call(
        filter_kernel,
        grid_spec=pltpu.PrefetchScalarGridSpec(
            num_scalar_prefetch=1,
            grid=(1,),
            in_specs=[vmem] * 3 + [pl.BlockSpec((1, 8, ROWS), lambda i, s: (s[0], 0, 0))],
            out_specs=pl.BlockSpec(memory_space=pl.ANY),
            scratch_shapes=[
                pltpu.VMEM(x.shape, jnp.float32),
                pltpu.VMEM((items, 9, 2, HALF, 2 * ROWS), jnp.bfloat16),
                pltpu.VMEM((items, 9, 2, HALF, ROWS), jnp.float32),
                pltpu.SemaphoreType.DMA((items + 1,)),
            ],
        ),
        out_shape=jax.ShapeDtypeStruct(x.shape, jnp.float32),
        compiler_params=pltpu.CompilerParams(vmem_limit_bytes=28 * 1024 * 1024),
        cost_estimate=pl.CostEstimate(
            flops=216 * HALF * HALF * ROWS * items,
            bytes_accessed=3_500_000 * items,
            transcendentals=0,
        ),
    )(place, x, jnp.asarray(matrix), jnp.asarray(columns), tables)


BESIDE = ((0, 3), (1, 2), (6, 5), (7, 4))
BEYOND = ((0, 4), (1, 5), (6, 2), (7, 3))


def lent(pairs, turn):
    return [
        (lon * N_LAT + polar, (lon ^ turn) * N_LAT + other)
        for lon in range(N_LON)
        for polar, other in pairs
    ]


def returned(pairs, turn):
    return [(j, i) for i, j in lent(pairs, turn)]


def partner(band, pairs):
    return sum(jnp.where(band == other, polar, 0) for polar, other in pairs).astype(jnp.int32)


def unused(*likes):
    return pl.pallas_call(
        lambda *outs: None,
        out_specs=[pl.BlockSpec(memory_space=pl.ANY)] * len(likes),
        out_shape=[jax.ShapeDtypeStruct(like.shape, like.dtype) for like in likes],
    )()


def shards(u_wind, v_wind, height):
    band = lax.axis_index("lat")
    is_polar = (band < N_LAT // 4) | (band >= N_LAT - N_LAT // 4)
    even = band % 2 == 0
    place = jnp.stack([band, band == N_LAT - 1, band == 0, is_polar, even]).astype(jnp.int32)
    tables = jnp.asarray(latitude_tables())
    fields = [jnp.swapaxes(x, 0, 1) for x in (height, u_wind, v_wind)]
    flat = [x.reshape(COLS * LEV, ROWS) for x in fields]
    first, second = pack(place, *flat)
    swap = [(i, i ^ 1) for i in range(N_LAT)]
    first = lax.ppermute(first, "lat", swap)
    routes = [(lon, i, lon, i + 1) for lon in range(N_LON) for i in range(1, N_LAT - 1, 2)]
    routes += [(lon, i + 1, lon, i) for lon, i, _, _ in routes]
    routes += [
        (lon, i, (lon + N_LON // 2) % N_LON, i) for lon in range(N_LON) for i in (0, N_LAT - 1)
    ]
    second = lax.ppermute(
        second,
        AXES,
        [(a * N_LAT + b, c * N_LAT + d) for a, b, c, d in routes],
    )
    def exchange(value):
        return lax.all_to_all(value, "lon", split_axis=0, concat_axis=0, tiled=True)

    def help_out(h_first, h_second):
        circles = exchange(jnp.concatenate([h_first, h_second], 0))
        lender = jnp.where(
            lax.axis_index("lon") < N_LON // 2, partner(band, BESIDE), partner(band, BEYOND)
        )
        smooth = polar_filter(lender.reshape(1), circles[:, None], tables)[:, 0]
        h = exchange(smooth)
        return h[: LEV // 2], h[LEV // 2 :]

    inputs = (place, *flat, first, second, tables)
    whole = jax.ShapeDtypeStruct((LEV, 2, TALL, ROWS), jnp.float32)
    half = jax.ShapeDtypeStruct((LEV // 2, TALL, ROWS), jnp.float32)
    own = jax.ShapeDtypeStruct((COLS * LEV, ROWS), jnp.float32)
    ends = jax.ShapeDtypeStruct((3, LEV, ROWS), jnp.float32)
    uv, h_first, h_second = lax.cond(
        is_polar,
        lambda *inputs: tuple(stencil(True, *inputs)),
        lambda *inputs: tuple(unused(whole, half, half)),
        *inputs,
    )

    h_first = lax.ppermute(h_first, AXES, lent(BESIDE, 0))
    h_second = lax.ppermute(h_second, AXES, lent(BEYOND, N_LON // 2))
    def beside(own_h, own_u, own_v, onward, back):
        me = lax.axis_index("lon")
        to = jnp.arange(N_LON).reshape(N_LON, 1, 1, 1)
        sent = jnp.where(to == (me + 1) % N_LON, onward, 0.0)
        got = exchange(jnp.where(to == (me - 1) % N_LON, back, sent))

        def of(source):
            return lax.dynamic_index_in_dim(got, source % N_LON, 0, keepdims=False)

        return own_h, own_u, own_v, of(me - 1), of(me + 1)

    circles, own_h, own_u, own_v, west, east = lax.cond(
        is_polar,
        lambda uv, *inputs: (
            polar_filter(place, exchange(uv), tables),
            *unused(own, own, own, ends, ends),
        ),
        lambda uv, *inputs: (*unused(uv), *beside(*stencil(False, *inputs))),
        uv, *inputs,
    )
    h_first, h_second, circles = lax.optimization_barrier((h_first, h_second, circles))
    h_first, h_second = lax.cond(
        is_polar, lambda *parts: tuple(unused(*parts)), help_out, h_first, h_second
    )
    h_first = lax.ppermute(h_first, AXES, returned(BESIDE, 0))
    h_second = lax.ppermute(h_second, AXES, returned(BEYOND, N_LON // 2))
    uv = lax.cond(is_polar, exchange, lambda like: unused(like)[0], circles)
    result = unpack(place, own_u, own_v, own_h, west, east, uv, h_first, h_second)
    return tuple(jnp.swapaxes(x.reshape(COLS, LEV, ROWS), 0, 1) for x in result)


def solution(mesh):
    placed = (P(None, "lon", "lat"),) * 3
    return jax.shard_map(shards, mesh=mesh, in_specs=placed, out_specs=placed, check_vma=False)
```
